128 devices in a mesh: dp: 4 (over z_lo, core), dap: 32 (over x, z_hi, y).
Axes of the slice: x: 4, y: 4, z: 4 (z_hi: 2, z_lo: 2; z = z_hi * 2 + z_lo), core: 2. Of those that a mesh axis runs over, the one named last changes fastest.
Arguments:
- alignment_state: bfloat16 [1024, 512, 256], P(('dp', 'dap')), parts along dimension 0, may hold values from -6 to 6
- token_index_grid: int32 [1024, 512], P(('dp', 'dap')), parts along dimension 0, may hold values from 0 to 22
- sequence_mask: int32 [1024], P('dp'), parts along dimension 0, may hold values from 0 to 1, as said below
- residue_mask: int32 [2048], P('dp'), parts along dimension 0, may hold values from 0 to 1, as said below
- pair_state: bfloat16 [2048, 512, 128], P(('dp', 'dap')), parts along dimension 0, may hold values from -6 to 6
- token_embedding_table: bfloat16 [23, 256], replicated, may hold values from -6 to 6
- pair_bias_weight: bfloat16 [128, 8], replicated, may hold values from -0.5 to 0.5
- row_query_weight: bfloat16 [256, 256], replicated, may hold values from -10 to 10
- row_key_weight: bfloat16 [256, 256], replicated, may hold values from -10 to 10
- row_value_weight: bfloat16 [256, 256], replicated, may hold values from -0.375 to 0.375
- row_gate_weight: bfloat16 [256, 256], replicated, may hold values from -0.375 to 0.375
- row_output_weight: bfloat16 [256, 256], replicated, may hold values from -0.375 to 0.375
- column_query_weight: bfloat16 [256, 256], replicated, may hold values from -10 to 10
- column_key_weight: bfloat16 [256, 256], replicated, may hold values from -10 to 10
- column_value_weight: bfloat16 [256, 256], replicated, may hold values from -0.375 to 0.375
- column_gate_weight: bfloat16 [256, 256], replicated, may hold values from -0.375 to 0.375
- column_output_weight: bfloat16 [256, 256], replicated, may hold values from -0.375 to 0.375
Outputs:
- msa_out: bfloat16 [1024, 512, 256], P('dp', 'dap'), parts along dimension 0
The draws below stay inside these ranges and needn't reach their ends.
There are 4 independent parts, one for each index of `dp`. The reference program is written for one: setup_inputs(seed, part) draws one part's arguments, and reference() takes and returns one part's arrays. A program takes and returns all parts, laid end to end along the dimension named above; an argument that names none is the same for every part. Nothing has to cross between parts.
Inputs may be any that keep to these rules, and one draw needn't show every extreme that they name: `sequence_mask`: entry 0 is 1 and the last entry is 0. `residue_mask`: entry 0 is 1 and the last entry is 0.
All inputs are finite; a program needn't handle non-finite values.
Results may differ from the reference program's by a relative error of at most 0.013.
Values may be sent and summed in bfloat16 or wider, within the bound.
A program may use at most 192 MiB of HBM per device.

```python
import math
import jax
import jax.numpy as jnp
from jax import lax

ALIGNMENT_WIDTH = 256
PAIR_CH = 128
HEADS = 8
HEAD_DIM = 32
TOKEN_KINDS = 23
SEQUENCE_COUNT = 256
RESIDUE_COUNT = 512


def shared_weight(key, random_offset):
    return jax.random.truncated_normal(jax.random.fold_in(key, random_offset), -4.0, 4.0, (ALIGNMENT_WIDTH, ALIGNMENT_WIDTH), jnp.float32) / math.sqrt(ALIGNMENT_WIDTH)


def fresh_weight(key):
    return jax.random.truncated_normal(key, -4.0, 4.0, (ALIGNMENT_WIDTH, ALIGNMENT_WIDTH), jnp.float32) / math.sqrt(ALIGNMENT_WIDTH)


def draw_row_query_weight(key, part):
    base = shared_weight(key, 101)
    return base.astype(jnp.bfloat16)


def draw_row_key_weight(key, part):
    key = jax.random.fold_in(key, 2)
    return fresh_weight(key).astype(jnp.bfloat16)


def draw_column_query_weight(key, part):
    base = shared_weight(key, 202)
    return base.astype(jnp.bfloat16)


def draw_column_key_weight(key, part):
    key = jax.random.fold_in(key, 4)
    return fresh_weight(key).astype(jnp.bfloat16)


def mask_line(key, count):
    coin_key = jax.random.fold_in(key, 11)
    span_key = jax.random.fold_in(key, 12)
    coins = jax.random.randint(coin_key, (count,), 0, 4)
    real_count = jax.random.randint(span_key, (), count // 2, count)
    places = jnp.arange(count)
    live = jnp.logical_and(coins < 3, places < real_count).astype(jnp.int32)
    live = jnp.where(places == count - 1, 0, live)
    return jnp.where(places == 0, 1, live).astype(jnp.int32)


def draw_residue_mask(key, part):
    key = jax.random.fold_in(key, 5)
    return mask_line(key, RESIDUE_COUNT)


def draw_sequence_mask(key, part):
    key = jax.random.fold_in(key, 6)
    return mask_line(key, SEQUENCE_COUNT)


def with_ends(entries, key, smallest, top_value):
    spot = [jax.random.randint(jax.random.fold_in(key, axis), (), 0, length) for axis, length in enumerate(entries.shape)]
    longest = entries.shape.index(max(entries.shape))
    neighbour = spot[:longest] + [(spot[longest] + 1) % entries.shape[longest]] + spot[longest + 1:]
    return entries.at[tuple(spot)].set(smallest).at[tuple(neighbour)].set(top_value)


def level_of(rng, extent, cuts, low, largest):
    loudness = 1.0
    for position, shards_of in cuts:
        draws = jax.random.uniform(jax.random.fold_in(jax.random.fold_in(rng, 6), position), (shards_of,), jnp.float32, low / len(cuts), largest / len(cuts))
        loudness = loudness * jnp.repeat(jnp.exp(draws), extent[position] // shards_of).reshape((-1,) + (1,) * (len(extent) - 1 - position))
    return loudness


def bell_draw(own_key, extent, spread, reach, pieces=(), kind=jnp.bfloat16):
    array = jax.random.normal(own_key, extent, jnp.float32) * spread
    if len(pieces) > 0:
        array = level_of(own_key, extent, pieces, -0.22, 0.18) * array
    return jnp.clip(array, min=-reach, max=reach).astype(kind)


def setup_inputs(seed: int = 0, part: int = 0) -> dict:
    splits = jax.random.split(jax.random.key(seed), 18)
    part_splits = jax.random.split(jax.random.fold_in(splits[17], part), 18)
    return {
        "alignment_state": bell_draw(part_splits[0], (SEQUENCE_COUNT, RESIDUE_COUNT, ALIGNMENT_WIDTH), 1.0, 6.0, ((0, 32),)),
        "token_index_grid": with_ends(jax.random.randint(part_splits[1], (SEQUENCE_COUNT, RESIDUE_COUNT), 0, TOKEN_KINDS), jax.random.fold_in(part_splits[1], 1), 0, TOKEN_KINDS - 1).astype(jnp.int32),
        "sequence_mask": draw_sequence_mask(jax.random.fold_in(jax.random.fold_in(splits[17], part), 71), part),
        "residue_mask": draw_residue_mask(jax.random.fold_in(jax.random.fold_in(splits[17], part), 71), part),
        "pair_state": bell_draw(part_splits[4], (RESIDUE_COUNT, RESIDUE_COUNT, PAIR_CH), 1.0, 6.0, ((0, 32),)),
        "token_embedding_table": bell_draw(splits[5], (TOKEN_KINDS, ALIGNMENT_WIDTH), 1.0, 6.0),
        "pair_bias_weight": bell_draw(splits[6], (PAIR_CH, HEADS), PAIR_CH ** -0.5, 0.5),
        "row_query_weight": draw_row_query_weight(jax.random.fold_in(splits[17], 71), part),
        "row_key_weight": draw_row_key_weight(jax.random.fold_in(splits[17], 71), part),
        "row_value_weight": bell_draw(splits[9], (ALIGNMENT_WIDTH, ALIGNMENT_WIDTH), ALIGNMENT_WIDTH ** -0.5, 0.375),
        "row_gate_weight": bell_draw(splits[10], (ALIGNMENT_WIDTH, ALIGNMENT_WIDTH), ALIGNMENT_WIDTH ** -0.5, 0.375),
        "row_output_weight": bell_draw(splits[11], (ALIGNMENT_WIDTH, ALIGNMENT_WIDTH), ALIGNMENT_WIDTH ** -0.5, 0.375),
        "column_query_weight": draw_column_query_weight(jax.random.fold_in(splits[17], 71), part),
        "column_key_weight": draw_column_key_weight(jax.random.fold_in(splits[17], 71), part),
        "column_value_weight": bell_draw(splits[14], (ALIGNMENT_WIDTH, ALIGNMENT_WIDTH), ALIGNMENT_WIDTH ** -0.5, 0.375),
        "column_gate_weight": bell_draw(splits[15], (ALIGNMENT_WIDTH, ALIGNMENT_WIDTH), ALIGNMENT_WIDTH ** -0.5, 0.375),
        "column_output_weight": bell_draw(splits[16], (ALIGNMENT_WIDTH, ALIGNMENT_WIDTH), ALIGNMENT_WIDTH ** -0.5, 0.375),
    }


EPSILON = 1e-05

def normalize(values):
    centered = values - lax.optimization_barrier(jnp.mean(values, axis=-1, keepdims=True))
    variance = lax.optimization_barrier(jnp.mean(centered * centered, axis=-1, keepdims=True))
    return centered * lax.rsqrt(variance + EPSILON)

def attend_line(normed, w_query, w_key, w_value, w_gate, w_out, bias_heads, key_mask):
    length = normed.shape[0]
    queries = (jnp.dot(normed, w_query, preferred_element_type=jnp.float32) * HEAD_DIM ** (-0.5)).astype(jnp.bfloat16)
    queries = queries.reshape(length, HEADS, HEAD_DIM)
    keyed = jnp.dot(normed, w_key, preferred_element_type=jnp.float32).astype(jnp.bfloat16).reshape(length, HEADS, HEAD_DIM)
    valued = jnp.dot(normed, w_value, preferred_element_type=jnp.float32).astype(jnp.bfloat16).reshape(length, HEADS, HEAD_DIM)
    scores = jnp.einsum('qhd,khd->hqk', queries.astype(jnp.float32), keyed.astype(jnp.float32))
    if bias_heads is not None:
        scores = scores + bias_heads.astype(jnp.float32)
    scores = jnp.where(key_mask[None, None, :] > 0, scores, -1000000000.0)
    attn_probs = jax.nn.softmax(scores, axis=-1).astype(jnp.bfloat16)
    attended = jnp.einsum('hqk,khd->qhd', attn_probs.astype(jnp.float32), valued.astype(jnp.float32))
    attended = attended.reshape(length, HEADS * HEAD_DIM)
    gating = jax.nn.sigmoid(jnp.dot(normed, w_gate, preferred_element_type=jnp.float32))
    gated_mix = (attended * gating).astype(jnp.bfloat16)
    return jnp.dot(gated_mix, w_out, preferred_element_type=jnp.float32)

def reference(alignment_state, token_index_grid, sequence_mask, residue_mask, pair_state, token_embedding_table, pair_bias_weight, row_query_weight, row_key_weight, row_value_weight, row_gate_weight, row_output_weight, column_query_weight, column_key_weight, column_value_weight, column_gate_weight, column_output_weight):
    token_indicator = jax.nn.one_hot(token_index_grid, TOKEN_KINDS, dtype=jnp.float32)
    token_embedded = alignment_state.astype(jnp.float32) + jnp.einsum('ulk,kg->ulg', token_indicator, token_embedding_table.astype(jnp.float32))
    row_normed = normalize(token_embedded).astype(jnp.bfloat16)
    pair_normed = normalize(pair_state.astype(jnp.float32)).astype(jnp.bfloat16)
    pair_bias = jnp.einsum('qkc,ch->hqk', pair_normed.astype(jnp.float32), pair_bias_weight.astype(jnp.float32)).astype(jnp.bfloat16)

    def row_line(line):
        return attend_line(line, row_query_weight, row_key_weight, row_value_weight, row_gate_weight, row_output_weight, pair_bias, residue_mask)
    row_update = lax.map(row_line, row_normed)
    updated = (token_embedded + row_update).astype(jnp.bfloat16)
    col_normed = normalize(updated.astype(jnp.float32)).astype(jnp.bfloat16)

    def col_line(line):
        return attend_line(line, column_query_weight, column_key_weight, column_value_weight, column_gate_weight, column_output_weight, None, sequence_mask)
    col_update = lax.map(col_line, jnp.transpose(col_normed, (1, 0, 2)))
    return (updated.astype(jnp.float32) + jnp.transpose(col_update, (1, 0, 2))).astype(jnp.bfloat16)
```

```python
import functools

import jax
import jax.numpy as jnp
from jax import lax
from jax.experimental import pallas as pl
from jax.experimental.pallas import tpu as pltpu
from jax.sharding import PartitionSpec as P

HEADS = 8
HEAD_DIM = 32
GROUP = 4
TOKEN_KINDS = 23
EPSILON = 1e-05
LOG2E = 1.4426950408889634
MASKED = -1e9
QUERY_ROWS = 128
VMEM_LIMIT = 60 * 1024 * 1024

NT = (((1,), (1,)), ((), ()))
TN = (((0,), (0,)), ((), ()))


def dot(a, b, dims=(((1,), (0,)), ((), ()))):
    return lax.dot_general(a, b, dims, preferred_element_type=jnp.float32)


def normalize(values):
    centered = values - jnp.mean(values, axis=-1, keepdims=True)
    variance = jnp.mean(centered * centered, axis=-1, keepdims=True)
    return centered * lax.rsqrt(variance + EPSILON)


def sigmoid(x):
    return 0.5 * jnp.tanh(0.5 * x) + 0.5


def lane_head(shape):
    return lax.broadcasted_iota(jnp.int32, shape, len(shape) - 1) // HEAD_DIM


def bias_kernel(pair_ref, weight_ref, out_ref):
    rows = pair_ref.shape[0]
    channels = pair_ref.shape[2]
    weight = weight_ref[...]
    averaging = jnp.full((channels, channels), 1.0 / channels, jnp.bfloat16)
    for row in range(rows):
        block = pair_ref[row]
        centered = block.astype(jnp.float32) - dot(block, averaging)
        variance = dot((centered * centered).astype(jnp.bfloat16), averaging)
        normed = (centered * lax.rsqrt(variance + EPSILON)).astype(jnp.bfloat16)
        projected = dot(weight, normed, (((0,), (1,)), ((), ())))
        out_ref[:, row, :] = projected.astype(jnp.bfloat16)


def pair_bias(pair_state, weight):
    rows, keys, channels = pair_state.shape
    return pl.pallas_call(
        bias_kernel,
        out_shape=jax.ShapeDtypeStruct((HEADS, rows, keys), jnp.bfloat16),
        in_specs=[pl.BlockSpec(memory_space=pltpu.VMEM)] * 2,
        out_specs=pl.BlockSpec(memory_space=pltpu.VMEM),
        compiler_params=pltpu.CompilerParams(vmem_limit_bytes=VMEM_LIMIT),
        name="pair_bias",
    )(pair_state, weight)


def store_keys(key_ref, index, keyed):
    lanes = lane_head((1, 128))
    for head in range(HEADS):
        part = keyed[:, 128 * (head // GROUP):128 * (head // GROUP + 1)]
        key_ref[index, head] = jnp.where(lanes == head % GROUP, part, 0.0).astype(jnp.bfloat16)


def store_values(value_ref, index, valued, live):
    lanes = lane_head((1, 128))
    for head in range(HEADS):
        part = valued[:, 128 * (head // GROUP):128 * (head // GROUP + 1)]
        mine = lanes == head % GROUP
        value_ref[index, head, :, 0:128] = jnp.where(mine, part, 0.0).astype(jnp.bfloat16)
        value_ref[index, head, :, 128:256] = jnp.where(mine, jnp.broadcast_to(live, part.shape), 0.0).astype(jnp.bfloat16)


def attend(queries, key_at, value_at, bias_at):
    halves = []
    for group in range(HEADS // GROUP):
        q = queries[:, 128 * group:128 * (group + 1)]
        total = None
        for inner in range(GROUP):
            head = group * GROUP + inner
            scores = dot(q, key_at(head), NT)
            if bias_at is not None:
                scores = scores + bias_at(head)
            top = jnp.max(scores, axis=-1, keepdims=True)
            probs = jnp.exp2(scores - top).astype(jnp.bfloat16)
            product = dot(probs, value_at(head))
            total = product if total is None else total + product
        halves.append(total[:, 0:128] / total[:, 128:256])
    return jnp.concatenate(halves, axis=1)


def row_kernel(
    state_ref, token_ref, mask_ref, bias_ref, table_ref,
    wq_ref, wk_ref, wv_ref, wg_ref, wo_ref,
    out_ref,
    embedded_ref, query_ref, key_ref, value_ref, gate_ref, wide_ref,
):
    sequences, residues, channels = state_ref.shape
    peers, _, rows_each, _ = bias_ref.shape

    @pl.loop(0, sequences)
    def _(s):
        tokens = token_ref[pl.ds(s, 1), :]
        kinds = lax.broadcasted_iota(jnp.int32, (TOKEN_KINDS, residues), 0)
        indicator = (kinds == tokens).astype(jnp.float32).astype(jnp.bfloat16)
        embedded = state_ref[s].astype(jnp.float32) + dot(indicator, table_ref[...], TN)
        embedded_ref[s] = embedded
        normed = normalize(embedded).astype(jnp.bfloat16)
        query_ref[s] = (dot(normed, wq_ref[...]) * (HEAD_DIM ** -0.5 * LOG2E)).astype(jnp.bfloat16)
        store_keys(key_ref, s, dot(normed, wk_ref[...]))
        store_values(value_ref, s, dot(normed, wv_ref[...]), jnp.ones((1, 1), jnp.float32))
        gate_ref[s] = sigmoid(dot(normed, wg_ref[...])).astype(jnp.bfloat16)

    live = mask_ref[...] > 0
    blocks = QUERY_ROWS // rows_each

    @pl.loop(0, residues // QUERY_ROWS)
    def _(chunk):
        for head in range(HEADS):
            part = bias_ref[pl.ds(chunk * blocks, blocks), head].reshape(QUERY_ROWS, residues)
            wide_ref[head] = jnp.where(live, part.astype(jnp.float32) * LOG2E, MASKED)

        @pl.loop(0, sequences)
        def _(s):
            rows = pl.ds(pl.multiple_of(chunk * QUERY_ROWS, QUERY_ROWS), QUERY_ROWS)
            attended = attend(
                query_ref[s, rows, :],
                lambda head: key_ref[s, head],
                lambda head: value_ref[s, head],
                lambda head: wide_ref[head],
            )
            mixed = (attended * gate_ref[s, rows, :].astype(jnp.float32)).astype(jnp.bfloat16)
            updated = (embedded_ref[s, rows, :] + dot(mixed, wo_ref[...])).astype(jnp.bfloat16)
            out_ref[pl.ds(chunk * blocks, blocks), s] = updated.reshape(blocks, rows_each, channels)


def row_attention(state, tokens, mask, bias, table, weights):
    sequences, residues, channels = state.shape
    peers, _, rows_each, _ = bias.shape
    return pl.pallas_call(
        row_kernel,
        out_shape=jax.ShapeDtypeStruct((peers, sequences, rows_each, channels), jnp.bfloat16),
        in_specs=[pl.BlockSpec(memory_space=pltpu.VMEM)] * 10,
        out_specs=pl.BlockSpec(memory_space=pltpu.VMEM),
        scratch_shapes=[
            pltpu.VMEM((sequences, residues, channels), jnp.float32),
            pltpu.VMEM((sequences, residues, channels), jnp.bfloat16),
            pltpu.VMEM((sequences, HEADS, residues, 128), jnp.bfloat16),
            pltpu.VMEM((sequences, HEADS, residues, 256), jnp.bfloat16),
            pltpu.VMEM((sequences, residues, channels), jnp.bfloat16),
            pltpu.VMEM((HEADS, QUERY_ROWS, residues), jnp.float32),
        ],
        compiler_params=pltpu.CompilerParams(vmem_limit_bytes=VMEM_LIMIT),
        name="row_attention",
    )(state, tokens, mask, bias, table, *weights)


def column_kernel(
    arrived_ref, mask_ref, wq_ref, wk_ref, wv_ref, wg_ref, wo_ref,
    out_ref,
    wide_ref, key_ref, value_ref,
):
    sequences, residues, channels = arrived_ref.shape
    halves = 8

    @pl.loop(0, halves)
    def _(i):
        rows = sequences // halves
        part = arrived_ref[pl.ds(pl.multiple_of(i * rows, rows), rows)]
        part = part.astype(jnp.float32).reshape(rows * residues, channels)
        for half in range(2):
            wide_ref[half, pl.ds(pl.multiple_of(i * rows * residues, rows * residues), rows * residues), :] = (
                part[:, 128 * half:128 * (half + 1)]
            )

    live = jnp.transpose(jnp.broadcast_to(mask_ref[...].astype(jnp.float32), (128, sequences)))
    live = jnp.concatenate([live, live], axis=1)

    @pl.loop(0, residues)
    def _(r):
        updated = jnp.concatenate(
            [wide_ref[half, pl.ds(r, sequences, stride=residues), :] for half in range(2)], axis=1
        )
        normed = normalize(updated).astype(jnp.bfloat16)
        queries = (dot(normed, wq_ref[...]) * (HEAD_DIM ** -0.5 * LOG2E)).astype(jnp.bfloat16)
        keyed = dot(normed, wk_ref[...])
        keyed = jnp.where(live > 0.0, keyed, keyed[0:1, :])
        store_keys(key_ref, 0, keyed)
        store_values(value_ref, 0, dot(normed, wv_ref[...]) * live, live[:, 0:128])
        gate = sigmoid(dot(normed, wg_ref[...]))
        attended = attend(
            queries, lambda head: key_ref[0, head], lambda head: value_ref[0, head], None
        )
        mixed = (attended * gate).astype(jnp.bfloat16)
        result = updated + dot(mixed, wo_ref[...])
        for half in range(2):
            wide_ref[half, pl.ds(r, sequences, stride=residues), :] = result[:, 128 * half:128 * (half + 1)]

    @pl.loop(0, halves)
    def _(i):
        rows = sequences // halves
        span = pl.ds(pl.multiple_of(i * rows * residues, rows * residues), rows * residues)
        part = jnp.concatenate([wide_ref[half, span, :] for half in range(2)], axis=1)
        out_ref[pl.ds(pl.multiple_of(i * rows, rows), rows)] = (
            part.astype(jnp.bfloat16).reshape(rows, residues, channels)
        )


def column_attention(arrived, mask, weights):
    sequences, residues, channels = arrived.shape
    return pl.pallas_call(
        column_kernel,
        out_shape=jax.ShapeDtypeStruct(arrived.shape, jnp.bfloat16),
        in_specs=[pl.BlockSpec(memory_space=pltpu.VMEM)] * 7,
        out_specs=pl.BlockSpec(memory_space=pltpu.VMEM),
        scratch_shapes=[
            pltpu.VMEM((2, sequences * residues, 128), jnp.float32),
            pltpu.VMEM((1, HEADS, sequences, 128), jnp.bfloat16),
            pltpu.VMEM((1, HEADS, sequences, 256), jnp.bfloat16),
        ],
        compiler_params=pltpu.CompilerParams(vmem_limit_bytes=VMEM_LIMIT),
        name="column_attention",
    )(arrived, mask, *weights)


def body(
    alignment_state,
    token_index_grid,
    sequence_mask,
    residue_mask,
    pair_state,
    token_embedding_table,
    pair_bias_weight,
    row_query_weight,
    row_key_weight,
    row_value_weight,
    row_gate_weight,
    row_output_weight,
    column_query_weight,
    column_key_weight,
    column_value_weight,
    column_gate_weight,
    column_output_weight,
):
    bias_local = pair_bias(pair_state, pair_bias_weight)
    bias = lax.all_gather(bias_local, "dap", axis=0)
    blocks = row_attention(
        alignment_state, token_index_grid, residue_mask[None, :], bias, token_embedding_table,
        (row_query_weight, row_key_weight, row_value_weight, row_gate_weight, row_output_weight),
    )
    arrived = lax.all_to_all(blocks, "dap", split_axis=0, concat_axis=0, tiled=True)
    peers, seqs, rows_each, channels = blocks.shape
    arrived = arrived.reshape(peers * seqs, rows_each, channels)
    return column_attention(
        arrived, sequence_mask[None, :],
        (column_query_weight, column_key_weight, column_value_weight, column_gate_weight,
         column_output_weight),
    )


def solution(mesh):
    split = P(("dp", "dap"), None, None)
    in_specs = (
        split, P(("dp", "dap"), None), P("dp"), P("dp"), split,
    ) + (P(),) * 12
    return jax.shard_map(
        body, mesh=mesh, in_specs=in_specs, out_specs=P("dp", "dap", None), check_vma=False
    )
```

```python
import functools

import jax
import jax.numpy as jnp
from jax import lax
from jax.experimental import pallas as pl
from jax.experimental.pallas import tpu as pltpu
from jax.sharding import PartitionSpec as P

HEADS = 8
HEAD_DIM = 32
GROUP = 4
TOKEN_KINDS = 23
EPSILON = 1e-05
LOG2E = 1.4426950408889634
MASKED = -1e9
QUERY_ROWS = 128
PIECE = 4
XS, ZS, YS = 4, 2, 4
MESH = pl.DeviceIdType.MESH
VMEM_LIMIT = 60 * 1024 * 1024

NT = (((1,), (1,)), ((), ()))
TN = (((0,), (0,)), ((), ()))


def dot(a, b, dims=(((1,), (0,)), ((), ()))):
    return lax.dot_general(a, b, dims, preferred_element_type=jnp.float32)


def normalize(values):
    centered = values - jnp.mean(values, axis=-1, keepdims=True)
    variance = jnp.mean(centered * centered, axis=-1, keepdims=True)
    return centered * lax.rsqrt(variance + EPSILON)


def sigmoid(x):
    return 0.5 * jnp.tanh(0.5 * x) + 0.5


def lane_head(shape):
    return lax.broadcasted_iota(jnp.int32, shape, len(shape) - 1) // HEAD_DIM


def store_keys(key_ref, index, keyed):
    lanes = lane_head((1, 128))
    for head in range(HEADS):
        part = keyed[:, 128 * (head // GROUP):128 * (head // GROUP + 1)]
        key_ref[index, head] = jnp.where(lanes == head % GROUP, part, 0.0).astype(jnp.bfloat16)


def store_values(value_ref, index, valued, live):
    lanes = lane_head((1, 128))
    for head in range(HEADS):
        part = valued[:, 128 * (head // GROUP):128 * (head // GROUP + 1)]
        mine = lanes == head % GROUP
        value_ref[index, head, :, 0:128] = jnp.where(mine, part, 0.0).astype(jnp.bfloat16)
        value_ref[index, head, :, 128:256] = jnp.where(mine, jnp.broadcast_to(live, part.shape), 0.0).astype(jnp.bfloat16)


def attend(queries, key_at, value_at, bias_at):
    halves = []
    for group in range(HEADS // GROUP):
        q = queries[:, 128 * group:128 * (group + 1)]
        total = None
        for inner in range(GROUP):
            head = group * GROUP + inner
            scores = dot(q, key_at(head), NT)
            if bias_at is not None:
                scores = scores + bias_at(head)
            top = jnp.max(scores, axis=-1, keepdims=True)
            probs = jnp.exp2(scores - top).astype(jnp.bfloat16)
            product = dot(probs, value_at(head))
            total = product if total is None else total + product
        halves.append(total[:, 0:128] / total[:, 128:256])
    return jnp.concatenate(halves, axis=1)


def gather_plan():
    def place(half, u, z, v):
        return (v % XS, z % ZS, u % YS) if half == 0 else (u % XS, z % ZS, v % YS)

    first, steps = [], []
    for half in range(2):
        own = place(half, 0, 0, 0)
        for target in ((0, 1, 0), (1, 0, 0), (-1, 0, 0), (0, 0, 1), (0, 0, -1)):
            first.append((half, own, place(half, *target)))
        for u in (0, 1, -1, 2):
            for z in range(2):
                for v in (0, 1, -1, 2):
                    if (u, z, v) == (0, 0, 0):
                        continue
                    block, to = place(half, u, z, v), []
                    if v == 0:
                        if u == 0:
                            to += [(1, 0, 0), (-1, 0, 0)]
                        if (u, z) == (-1, 0):
                            to.append((1, 0, 0))
                        if (u, z) == (1, 1):
                            to.append((-1, 0, 0))
                        to += [(0, 0, 1), (0, 0, -1)]
                    if (z, v) == (0, -1):
                        to.append((0, 0, 1))
                    if (z, v) == (1, 1):
                        to.append((0, 0, -1))
                    hops = abs(u) + abs(v) + 1.5 * z
                    rank = (0, 1, 3, 2)[block[0]]
                    sends = [(half, block, place(half, *t)) for t in to]
                    steps.append((hops + 0.5 * rank + (0 if sends else 0.75), rank, half, block, sends))
    steps.sort(key=lambda step: step[:4])
    return first, [(step[1], (step[2], step[3]), step[4]) for step in steps]


def fill_slots(steps):
    slots, place = {}, 0
    room = [("project", s, 4) for s in range(8)]
    room += [(chunk, s, 2) for chunk in range(2) for s in range(8)]
    for stage, s, count in room:
        taken = steps[place:place + count]
        place += len(taken)
        slots[stage, s] = taken
    moved = {}
    order = ["project", 0, 1, 2]
    for chunk in range(3):
        late = []
        for (stage, s), taken in slots.items():
            if order.index(stage) > chunk:
                late += [step for step in taken if step[0] <= chunk]
                slots[stage, s] = [step for step in taken if step[0] > chunk]
        moved[chunk] = late
    return slots, moved


def row_kernel(
    pair_ref, pair_weight_ref, state_ref, token_ref, mask_ref, table_ref,
    wq_ref, wk_ref, wv_ref, wg_ref, wo_ref,
    arrived_ref,
    bias_ref, embedded_ref, query_ref, key_ref, value_ref, gate_ref, wide_ref, updated_ref,
    gather_send, gather_recv, turn_send, turn_recv, own_sem,
):
    sequences, residues, channels = state_ref.shape
    peers, _, rows_each, _ = bias_ref.shape
    me = lax.axis_index("dap")
    x, z, y = me // (ZS * YS), (me // YS) % ZS, me % YS

    def at(offset):
        dx, dz, dy = offset
        return (((x + dx) % XS) * ZS + (z + dz) % ZS) * YS + (y + dy) % YS

    barrier = pltpu.get_barrier_semaphore()
    for step in range(1, peers):
        pl.semaphore_signal(
            barrier, inc=1, device_id={"dap": (me + step) % peers}, device_id_type=MESH
        )

    pair_channels = pair_ref.shape[2]
    averaging = jnp.full((pair_channels, pair_channels), 1.0 / pair_channels, jnp.bfloat16)
    spread = jnp.transpose(pair_weight_ref[...].astype(jnp.float32))
    spread = jnp.broadcast_to(spread[:, None, :], (HEADS, rows_each, pair_channels))
    spread = spread.reshape(HEADS * rows_each, pair_channels)
    row_of = lax.broadcasted_iota(jnp.int32, spread.shape, 0) % rows_each
    total = None
    for row in range(rows_each):
        block = pair_ref[row]
        centered = block.astype(jnp.float32) - dot(block, averaging)
        variance = dot((centered * centered).astype(jnp.bfloat16), averaging)
        normed = (centered * lax.rsqrt(variance + EPSILON)).astype(jnp.bfloat16)
        weight = jnp.where(row_of == row, spread, 0.0).astype(jnp.bfloat16)
        product = dot(weight, normed, NT)
        total = product if total is None else total + product
    bias_ref[me] = total.astype(jnp.bfloat16).reshape(HEADS, rows_each, residues)

    pl.semaphore_wait(barrier, peers - 1)

    first, steps = gather_plan()
    sends = first + [send for step in steps for send in step[2]]
    number = {send: i for i, send in enumerate(sends)}

    def gather_copy(half, block, target, index):
        part = bias_ref.at[block, pl.ds(half * (HEADS // 2), HEADS // 2)]
        return pltpu.make_async_remote_copy(
            src_ref=part, dst_ref=part,
            send_sem=gather_send.at[index], recv_sem=gather_recv.at[half, block],
            device_id={"dap": target}, device_id_type=MESH,
        )

    def start(send):
        half, block, target = send
        gather_copy(half, at(block), at(target), number[send]).start()

    def run(steps):
        for _, (half, block), sends in steps:
            gather_copy(half, at(block), at((0, 1, 0)), 0).wait_recv()
            for send in sends:
                start(send)

    for send in first:
        start(send)
    slots, moved = fill_slots(steps)

    @pl.loop(0, sequences)
    def _(s):
        tokens = token_ref[pl.ds(s, 1), :]
        kinds = lax.broadcasted_iota(jnp.int32, (TOKEN_KINDS, residues), 0)
        indicator = (kinds == tokens).astype(jnp.float32).astype(jnp.bfloat16)
        embedded = state_ref[s].astype(jnp.float32) + dot(indicator, table_ref[...], TN)
        embedded_ref[s] = embedded
        normed = normalize(embedded).astype(jnp.bfloat16)
        query_ref[s] = (dot(normed, wq_ref[...]) * (HEAD_DIM ** -0.5 * LOG2E)).astype(jnp.bfloat16)
        store_keys(key_ref, s, dot(normed, wk_ref[...]))
        store_values(value_ref, s, dot(normed, wv_ref[...]), jnp.ones((1, 1), jnp.float32))
        gate_ref[s] = sigmoid(dot(normed, wg_ref[...])).astype(jnp.bfloat16)
        for k in range(8):
            if slots["project", k]:
                pl.when(s == k)(functools.partial(run, slots["project", k]))

    live = mask_ref[...] > 0
    blocks = QUERY_ROWS // rows_each

    def turn_copy(target, slot, piece):
        span = pl.ds(piece * PIECE, PIECE)
        return pltpu.make_async_remote_copy(
            src_ref=updated_ref.at[target, span], dst_ref=arrived_ref.at[slot, span],
            send_sem=turn_send.at[target, piece], recv_sem=turn_recv.at[slot, piece],
            device_id={"dap": target}, device_id_type=MESH,
        )

    def own_copy(piece):
        span = pl.ds(piece * PIECE, PIECE)
        return pltpu.make_async_copy(
            updated_ref.at[me, span], arrived_ref.at[me, span], own_sem.at[piece]
        )

    @pl.loop(0, XS)
    def _(chunk):
        far = (chunk * (chunk + 1) // 2) % XS
        cx = (x + far) % XS
        for k in range(3):
            if moved[k]:
                pl.when(chunk == k)(functools.partial(run, moved[k]))
        for head in range(HEADS):
            part = bias_ref[pl.ds(cx * blocks, blocks), head].reshape(QUERY_ROWS, residues)
            wide_ref[head] = jnp.where(live, part.astype(jnp.float32) * LOG2E, MASKED)

        @pl.loop(0, sequences)
        def _(s):
            rows = pl.ds(pl.multiple_of(cx * QUERY_ROWS, QUERY_ROWS), QUERY_ROWS)
            attended = attend(
                query_ref[s, rows, :],
                lambda head: key_ref[s, head],
                lambda head: value_ref[s, head],
                lambda head: wide_ref[head],
            )
            mixed = (attended * gate_ref[s, rows, :].astype(jnp.float32)).astype(jnp.bfloat16)
            updated = (embedded_ref[s, rows, :] + dot(mixed, wo_ref[...])).astype(jnp.bfloat16)
            updated_ref[pl.ds(cx * blocks, blocks), s] = updated.reshape(blocks, rows_each, channels)
            for c in range(2):
                for k in range(8):
                    if slots[c, k]:
                        pl.when((chunk == c) & (s == k))(functools.partial(run, slots[c, k]))

            @pl.when(s % PIECE == PIECE - 1)
            def _():
                piece = s // PIECE
                for j in range(blocks):
                    target = (cx * ZS + (z + j // YS) % ZS) * YS + (y + j) % YS
                    if j == 0:
                        @pl.when(chunk == 0)
                        def _():
                            own_copy(piece).start()

                        @pl.when(chunk > 0)
                        def _():
                            turn_copy(target, me, piece).start()
                    else:
                        turn_copy(target, me, piece).start()

    for send in sends:
        half, block, target = send
        gather_copy(half, at(block), at(target), number[send]).wait_send()

    @pl.loop(1, peers)
    def _(step):
        other = (me + step) % peers
        for piece in range(sequences // PIECE):
            turn_copy(other, other, piece).wait_send()
            turn_copy(other, other, piece).wait_recv()

    for piece in range(sequences // PIECE):
        own_copy(piece).wait()


def row_attention(pair_state, pair_weight, state, tokens, mask, table, weights):
    sequences, residues, channels = state.shape
    rows_each = pair_state.shape[0]
    peers = XS * ZS * YS
    block = (peers, sequences, rows_each, channels)
    return pl.pallas_call(
        row_kernel,
        out_shape=jax.ShapeDtypeStruct(block, jnp.bfloat16),
        in_specs=[pl.BlockSpec(memory_space=pltpu.VMEM)] * 11,
        out_specs=pl.BlockSpec(memory_space=pl.ANY),
        scratch_shapes=[
            pltpu.VMEM((peers, HEADS, rows_each, residues), jnp.bfloat16),
            pltpu.VMEM((sequences, residues, channels), jnp.float32),
            pltpu.VMEM((sequences, residues, channels), jnp.bfloat16),
            pltpu.VMEM((sequences, HEADS, residues, 128), jnp.bfloat16),
            pltpu.VMEM((sequences, HEADS, residues, 256), jnp.bfloat16),
            pltpu.VMEM((sequences, residues, channels), jnp.bfloat16),
            pltpu.VMEM((HEADS, QUERY_ROWS, residues), jnp.float32),
            pltpu.VMEM(block, jnp.bfloat16),
            pltpu.SemaphoreType.DMA((62,)),
            pltpu.SemaphoreType.DMA((2, peers)),
            pltpu.SemaphoreType.DMA((peers, sequences // PIECE)),
            pltpu.SemaphoreType.DMA((peers, sequences // PIECE)),
            pltpu.SemaphoreType.DMA((sequences // PIECE,)),
        ],
        compiler_params=pltpu.CompilerParams(
            vmem_limit_bytes=VMEM_LIMIT, collective_id=0, has_side_effects=True
        ),
        name="row_attention",
    )(pair_state, pair_weight, state, tokens, mask, table, *weights)


def column_kernel(
    arrived_ref, mask_ref, wq_ref, wk_ref, wv_ref, wg_ref, wo_ref,
    out_ref,
    wide_ref, key_ref, value_ref,
):
    sequences, residues, channels = arrived_ref.shape
    halves = 8

    @pl.loop(0, halves)
    def _(i):
        rows = sequences // halves
        part = arrived_ref[pl.ds(pl.multiple_of(i * rows, rows), rows)]
        part = part.astype(jnp.float32).reshape(rows * residues, channels)
        for half in range(2):
            wide_ref[half, pl.ds(pl.multiple_of(i * rows * residues, rows * residues), rows * residues), :] = (
                part[:, 128 * half:128 * (half + 1)]
            )

    live = jnp.transpose(jnp.broadcast_to(mask_ref[...].astype(jnp.float32), (128, sequences)))
    live = jnp.concatenate([live, live], axis=1)

    @pl.loop(0, residues)
    def _(r):
        updated = jnp.concatenate(
            [wide_ref[half, pl.ds(r, sequences, stride=residues), :] for half in range(2)], axis=1
        )
        normed = normalize(updated).astype(jnp.bfloat16)
        queries = (dot(normed, wq_ref[...]) * (HEAD_DIM ** -0.5 * LOG2E)).astype(jnp.bfloat16)
        keyed = dot(normed, wk_ref[...])
        keyed = jnp.where(live > 0.0, keyed, keyed[0:1, :])
        store_keys(key_ref, 0, keyed)
        store_values(value_ref, 0, dot(normed, wv_ref[...]) * live, live[:, 0:128])
        gate = sigmoid(dot(normed, wg_ref[...]))
        attended = attend(
            queries, lambda head: key_ref[0, head], lambda head: value_ref[0, head], None
        )
        mixed = (attended * gate).astype(jnp.bfloat16)
        result = updated + dot(mixed, wo_ref[...])
        for half in range(2):
            wide_ref[half, pl.ds(r, sequences, stride=residues), :] = result[:, 128 * half:128 * (half + 1)]

    @pl.loop(0, halves)
    def _(i):
        rows = sequences // halves
        span = pl.ds(pl.multiple_of(i * rows * residues, rows * residues), rows * residues)
        part = jnp.concatenate([wide_ref[half, span, :] for half in range(2)], axis=1)
        out_ref[pl.ds(pl.multiple_of(i * rows, rows), rows)] = (
            part.astype(jnp.bfloat16).reshape(rows, residues, channels)
        )


def column_attention(arrived, mask, weights):
    sequences, residues, channels = arrived.shape
    return pl.pallas_call(
        column_kernel,
        out_shape=jax.ShapeDtypeStruct(arrived.shape, jnp.bfloat16),
        in_specs=[pl.BlockSpec(memory_space=pltpu.VMEM)] * 7,
        out_specs=pl.BlockSpec(memory_space=pltpu.VMEM),
        scratch_shapes=[
            pltpu.VMEM((2, sequences * residues, 128), jnp.float32),
            pltpu.VMEM((1, HEADS, sequences, 128), jnp.bfloat16),
            pltpu.VMEM((1, HEADS, sequences, 256), jnp.bfloat16),
        ],
        compiler_params=pltpu.CompilerParams(vmem_limit_bytes=VMEM_LIMIT),
        name="column_attention",
    )(arrived, mask, *weights)


def body(
    alignment_state,
    token_index_grid,
    sequence_mask,
    residue_mask,
    pair_state,
    token_embedding_table,
    pair_bias_weight,
    row_query_weight,
    row_key_weight,
    row_value_weight,
    row_gate_weight,
    row_output_weight,
    column_query_weight,
    column_key_weight,
    column_value_weight,
    column_gate_weight,
    column_output_weight,
):
    arrived = row_attention(
        pair_state, pair_bias_weight, alignment_state, token_index_grid, residue_mask[None, :],
        token_embedding_table,
        (row_query_weight, row_key_weight, row_value_weight, row_gate_weight, row_output_weight),
    )
    peers, seqs, rows_each, channels = arrived.shape
    arrived = arrived.reshape(peers * seqs, rows_each, channels)
    return column_attention(
        arrived, sequence_mask[None, :],
        (column_query_weight, column_key_weight, column_value_weight, column_gate_weight,
         column_output_weight),
    )


def solution(mesh):
    split = P(("dp", "dap"), None, None)
    in_specs = (
        split, P(("dp", "dap"), None), P("dp"), P("dp"), split,
    ) + (P(),) * 12
    return jax.shard_map(
        body, mesh=mesh, in_specs=in_specs, out_specs=P("dp", "dap", None), check_vma=False
    )
```

```python
import functools

import jax
import jax.numpy as jnp
from jax import lax
from jax.experimental import pallas as pl
from jax.experimental.pallas import tpu as pltpu
from jax.sharding import PartitionSpec as P

HEADS = 8
HEAD_DIM = 32
GROUP = 4
TOKEN_KINDS = 23
EPSILON = 1e-05
LOG2E = 1.4426950408889634
MASKED = -1e9
ROWS = 8
PIECE = 2
COLUMNS = 2
LATER = 2.5
PROJECT_STEPS = (6, 8, 8, 8, 8, 8, 8, 8)
ATTEND_STEPS = (20, 20, 22, 0)
XS, ZS, YS = 4, 2, 4
MESH = pl.DeviceIdType.MESH
VMEM_LIMIT = 60 * 1024 * 1024

NT = (((1,), (1,)), ((), ()))
TN = (((0,), (0,)), ((), ()))


def dot(a, b, dims=(((1,), (0,)), ((), ()))):
    return lax.dot_general(a, b, dims, preferred_element_type=jnp.float32)


def normalize(values):
    centered = values - jnp.mean(values, axis=-1, keepdims=True)
    variance = jnp.mean(centered * centered, axis=-1, keepdims=True)
    return centered * lax.rsqrt(variance + EPSILON)


def sigmoid(x):
    return 0.5 * jnp.tanh(0.5 * x) + 0.5


def lane_head(shape):
    return lax.broadcasted_iota(jnp.int32, shape, len(shape) - 1) // HEAD_DIM


def head_lanes(inner):
    return (lane_head((1, 128)) == inner).astype(jnp.float32).astype(jnp.bfloat16)


def attend(queries, key_at, value_at, ones_at, bias_at):
    halves = []
    for group in range(HEADS // GROUP):
        q = queries[:, 128 * group:128 * (group + 1)]
        keyed, valued = key_at(group), value_at(group)
        all_probs, all_values = [], []
        for inner in range(GROUP):
            mine = head_lanes(inner)
            scores = dot(q, keyed * mine, NT)
            if bias_at is not None:
                scores = scores + bias_at(group * GROUP + inner)
            top = jnp.max(scores, axis=-1, keepdims=True)
            all_probs.append(jnp.exp2(scores - top).astype(jnp.bfloat16))
            all_values.append(jnp.concatenate([valued * mine, ones_at(inner)], axis=1))
        total = dot(jnp.concatenate(all_probs, axis=1), jnp.concatenate(all_values, axis=0))
        halves.append(total[:, 0:128] / total[:, 128:256])
    return jnp.concatenate(halves, axis=1)


def gather_plan():
    def place(half, u, z, v):
        return (v % XS, z % ZS, u % YS) if half == 0 else (u % XS, z % ZS, v % YS)

    first, steps = [], []
    for rows in range(2):
        for half in range(2):
            part = (rows, half)
            for target in ((0, 1, 0), (1, 0, 0), (-1, 0, 0), (0, 0, 1), (0, 0, -1)):
                first.append((part, (0, 0, 0), place(half, *target)))
            for u in (0, 1, -1, 2):
                for z in range(2):
                    for v in (0, 1, -1, 2):
                        if (u, z, v) == (0, 0, 0):
                            continue
                        to = []
                        if v == 0:
                            if u == 0:
                                to += [(1, 0, 0), (-1, 0, 0)]
                            if (u, z) == (-1, 0):
                                to.append((1, 0, 0))
                            if (u, z) == (1, 1):
                                to.append((-1, 0, 0))
                            to += [(0, 0, 1), (0, 0, -1)]
                        if (z, v) == (0, -1):
                            to.append((0, 0, 1))
                        if (z, v) == (1, 1):
                            to.append((0, 0, -1))
                        hops = abs(u) + abs(v) + 1.5 * z
                        order = hops + LATER * rows + (0 if to else 0.75)
                        steps.append((order, part, place(half, u, z, v), [place(half, *t) for t in to]))
    steps.sort(key=lambda step: step[:3])
    return first, [step[1:] for step in steps]


def fill_slots(steps):
    slots, place = {}, 0
    room = [("project", s, n) for s, n in enumerate(PROJECT_STEPS)]
    room += [("attend", s, n) for s, n in enumerate(ATTEND_STEPS)]
    for stage, s, count in room:
        slots[stage, s] = steps[place:place + count]
        place += count
    rest = steps[place:]
    early = []
    for (stage, s), taken in slots.items():
        if stage == "attend":
            early += [step for step in taken if step[0][0] == 0]
            slots[stage, s] = [step for step in taken if step[0][0] == 1]
    early += [step for step in rest if step[0][0] == 0]
    return slots, early, [step for step in rest if step[0][0] == 1]


def kernel(
    pair_ref, pair_weight_ref, state_ref, token_ref, residue_mask_ref, sequence_mask_ref, table_ref,
    row_wq, row_wk, row_wv, row_wg, row_wo, col_wq, col_wk, col_wv, col_wg, col_wo,
    out_ref,
    local_ref, bias_ref, embedded_ref, query_ref, key_ref, value_ref, gate_ref, wide_ref,
    updated_ref, arrived_ref, col_query, col_key, col_value, col_gate, live_ref, result_ref,
    local_sem, gather_send, gather_recv, turn_send, turn_recv,
):
    sequences, residues, channels = local_ref.shape
    rows_each, _, pair_channels = pair_ref.shape
    peers = residues // rows_each
    me = lax.axis_index("dap")
    x, z, y = me // (ZS * YS), (me // YS) % ZS, me % YS

    def at(offset):
        dx, dz, dy = offset
        return (((x + dx) % XS) * ZS + (z + dz) % ZS) * YS + (y + dy) % YS

    load = pltpu.make_async_copy(state_ref, local_ref, local_sem)
    load.start()
    barrier = pltpu.get_barrier_semaphore()
    for step in range(1, peers):
        pl.semaphore_signal(
            barrier, inc=1, device_id={"dap": (me + step) % peers}, device_id_type=MESH
        )

    first, steps = gather_plan()
    sends = first + [(part, block, target) for part, block, to in steps for target in to]
    number = {send: i for i, send in enumerate(sends)}

    def gather_copy(part, block, target, index):
        rows, half = part
        piece = bias_ref.at[rows, block, pl.ds(half * (HEADS // 2) * ROWS, HEADS // 2 * ROWS)]
        return pltpu.make_async_remote_copy(
            src_ref=piece, dst_ref=piece,
            send_sem=gather_send.at[index], recv_sem=gather_recv.at[rows, half, block],
            device_id={"dap": target}, device_id_type=MESH,
        )

    def start(send):
        part, block, target = send
        gather_copy(part, at(block), at(target), number[send]).start()

    def run(steps):
        for part, block, to in steps:
            gather_copy(part, at(block), at((0, 1, 0)), 0).wait_recv()
            for target in to:
                start((part, block, target))

    averaging = jnp.full((pair_channels, pair_channels), 1.0 / pair_channels, jnp.bfloat16)
    spread = pair_weight_ref[...].astype(jnp.float32)
    spread = jnp.broadcast_to(spread[:, None, :], (HEADS, ROWS, pair_channels))
    spread = spread.reshape(HEADS * ROWS, pair_channels)
    row_of = lax.broadcasted_iota(jnp.int32, spread.shape, 0) % ROWS
    for rows in range(2):
        total = None
        for row in range(ROWS):
            block = pair_ref[rows * ROWS + row]
            centered = block.astype(jnp.float32) - dot(block, averaging)
            variance = dot((centered * centered).astype(jnp.bfloat16), averaging)
            normed = (centered * lax.rsqrt(variance + EPSILON)).astype(jnp.bfloat16)
            weight = jnp.where(row_of == row, spread, 0.0).astype(jnp.bfloat16)
            product = dot(weight, normed, NT)
            total = product if total is None else total + product
        bias_ref[rows, me] = total.astype(jnp.bfloat16)
        if rows == 0:
            pl.semaphore_wait(barrier, peers - 1)
        for send in first:
            if send[0][0] == rows:
                start(send)

    slots, early, rest = fill_slots(steps)
    load.wait()

    def by_half(values):
        return jnp.swapaxes(values.reshape(peers, 2, ROWS, channels), 0, 1).reshape(
            2, peers * ROWS, channels
        )

    @pl.loop(0, sequences)
    def _(s):
        tokens = token_ref[pl.ds(s, 1), :]
        kinds = lax.broadcasted_iota(jnp.int32, (TOKEN_KINDS, residues), 0)
        indicator = (kinds == tokens).astype(jnp.float32).astype(jnp.bfloat16)
        embedded = local_ref[s].astype(jnp.float32) + dot(indicator, table_ref[...], TN)
        embedded_ref[s] = by_half(embedded)
        normed = normalize(embedded).astype(jnp.bfloat16)
        queries = dot(normed, row_wq[...]) * (HEAD_DIM ** -0.5 * LOG2E)
        query_ref[s] = by_half(queries).astype(jnp.bfloat16)
        key_ref[s] = dot(normed, row_wk[...]).astype(jnp.bfloat16)
        value_ref[s] = dot(normed, row_wv[...]).astype(jnp.bfloat16)
        gate_ref[s] = by_half(sigmoid(dot(normed, row_wg[...]))).astype(jnp.bfloat16)
        for k in range(sequences):
            if slots["project", k]:
                pl.when(s == k)(functools.partial(run, slots["project", k]))

    real = residue_mask_ref[...] > 0
    pairs = sequences // 2
    pieces = pairs // PIECE

    def turn_copy(rows, target, slot, piece):
        span = pl.ds(piece * PIECE, PIECE)
        return pltpu.make_async_remote_copy(
            src_ref=updated_ref.at[rows, target, span], dst_ref=arrived_ref.at[rows, slot, span],
            send_sem=turn_send.at[rows, target, piece], recv_sem=turn_recv.at[rows, slot, piece],
            device_id={"dap": target}, device_id_type=MESH,
        )

    run(early)

    @pl.loop(0, 2)
    def _(rows):
        if rest:
            pl.when(rows == 1)(functools.partial(run, rest))
        for head in range(0, HEADS, 2):
            both = bias_ref[rows, :, ROWS * head:ROWS * (head + 2), :].astype(jnp.float32) * LOG2E
            for i in range(2):
                part = both[:, ROWS * i:ROWS * (i + 1), :].reshape(peers * ROWS, residues)
                wide_ref[head + i] = jnp.where(real, part, MASKED)

        @pl.loop(0, pairs)
        def _(p):
            results = []
            for i in range(2):
                s = 2 * p + i
                attended = attend(
                    query_ref[s, rows],
                    lambda g: key_ref[s, :, 128 * g:128 * (g + 1)],
                    lambda g: value_ref[s, :, 128 * g:128 * (g + 1)],
                    lambda inner: jnp.broadcast_to(head_lanes(inner), (residues, 128)),
                    lambda head: wide_ref[head],
                )
                mixed = (attended * gate_ref[s, rows].astype(jnp.float32)).astype(jnp.bfloat16)
                updated = embedded_ref[s, rows] + dot(mixed, row_wo[...])
                results.append(updated.reshape(peers, ROWS, channels))
            updated_ref[rows, :, p] = jnp.concatenate(results, axis=1).astype(jnp.bfloat16)
            arrived_ref[rows, me, p] = updated_ref[rows, me, p]
            for k in range(pairs):
                if slots["attend", k]:
                    pl.when((rows == 0) & (p == k))(functools.partial(run, slots["attend", k]))

            @pl.when(p % PIECE == PIECE - 1)
            def _():
                for step in range(1, peers):
                    turn_copy(rows, (me + step) % peers, me, p // PIECE).start()

    tokens = 512
    lines = tokens // ROWS
    sources = lines // sequences
    everyone = peers * sequences
    real = jnp.broadcast_to(sequence_mask_ref[...].astype(jnp.float32), (128, everyone))
    real = jnp.transpose(real)
    for inner in range(GROUP):
        live_ref[inner] = real.astype(jnp.bfloat16) * head_lanes(inner)
    real = jnp.concatenate([real, real], axis=1)

    for rows in range(2):
        def arrivals(i):
            part = arrived_ref[rows, pl.ds(i * sources, sources)]
            return part.astype(jnp.float32).reshape(tokens, channels)

        def span_of(i):
            return pl.ds(pl.multiple_of(i * tokens, tokens), tokens)

        @pl.loop(0, peers // sources)
        def _(i):
            for j in range(sources):
                source = i * sources + j

                @pl.when(source != me)
                def _():
                    for piece in range(pieces):
                        turn_copy(rows, source, source, piece).wait_recv()
            span = span_of(i)
            normed = normalize(arrivals(i)).astype(jnp.bfloat16)
            queries = dot(normed, col_wq[...]) * (HEAD_DIM ** -0.5 * LOG2E)
            keyed = dot(normed, col_wk[...])
            valued = dot(normed, col_wv[...])
            for half in range(2):
                lanes = slice(128 * half, 128 * (half + 1))
                col_query[half, span, :] = queries[:, lanes]
                col_key[half, span, :] = keyed[:, lanes]
                col_value[half, span, :] = valued[:, lanes]
            col_gate[span, :] = sigmoid(dot(normed, col_wg[...])).astype(jnp.bfloat16)

        @pl.loop(0, ROWS // COLUMNS)
        def _(i):
            spans = [pl.ds(i * COLUMNS + j, everyone, stride=ROWS) for j in range(COLUMNS)]

            def line(ref, span):
                return jnp.concatenate([ref[half, span, :] for half in range(2)], axis=1)

            loaded = [[line(ref, span) for ref in (col_query, col_key, col_value)] for span in spans]
            results = []
            for queries, keyed, valued in loaded:
                keyed = jnp.where(real > 0.0, keyed, keyed[0:1, :]).astype(jnp.bfloat16)
                valued = (valued * real).astype(jnp.bfloat16)
                results.append(attend(
                    queries.astype(jnp.bfloat16),
                    lambda g: keyed[:, 128 * g:128 * (g + 1)],
                    lambda g: valued[:, 128 * g:128 * (g + 1)],
                    lambda inner: live_ref[inner],
                    None,
                ))
            for span, attended in zip(spans, results):
                for half in range(2):
                    col_query[half, span, :] = attended[:, 128 * half:128 * (half + 1)]

        @pl.loop(0, peers // sources)
        def _(i):
            span = span_of(i)
            attended = jnp.concatenate([col_query[half, span, :] for half in range(2)], axis=1)
            mixed = (attended * col_gate[span, :].astype(jnp.float32)).astype(jnp.bfloat16)
            result = arrivals(i) + dot(mixed, col_wo[...])
            if rows == 0:
                result_ref[span, :] = result
            else:
                both = [result_ref[span, :], result]
                both = [part.reshape(lines, ROWS, channels) for part in both]
                out_ref[pl.ds(pl.multiple_of(i * lines, lines), lines)] = (
                    jnp.concatenate(both, axis=1).astype(jnp.bfloat16)
                )

    for send in sends:
        part, block, target = send
        gather_copy(part, at(block), at(target), number[send]).wait_send()

    @pl.loop(1, peers)
    def _(step):
        for rows in range(2):
            for piece in range(pieces):
                turn_copy(rows, (me + step) % peers, me, piece).wait_send()


def both_attentions(pair_state, pair_weight, state, tokens, residue_mask, sequence_mask, table, weights):
    sequences, residues, channels = state.shape
    rows_each = pair_state.shape[0]
    peers = residues // rows_each
    everyone = peers * sequences
    pairs = sequences // 2
    block = (2, peers, pairs, 2 * ROWS, channels)
    first, steps = gather_plan()
    count = len(first) + sum(len(step[2]) for step in steps)
    whole = pl.BlockSpec(memory_space=pltpu.VMEM)
    bf16, f32 = jnp.bfloat16, jnp.float32
    return pl.pallas_call(
        kernel,
        out_shape=jax.ShapeDtypeStruct((everyone, rows_each, channels), bf16),
        in_specs=[whole] * 2 + [pl.BlockSpec(memory_space=pl.ANY)] + [whole] * 14,
        out_specs=whole,
        scratch_shapes=[
            pltpu.VMEM((sequences, residues, channels), bf16),
            pltpu.VMEM((2, peers, HEADS * ROWS, residues), bf16),
            pltpu.VMEM((sequences, 2, peers * ROWS, channels), f32),
            pltpu.VMEM((sequences, 2, peers * ROWS, channels), bf16),
            pltpu.VMEM((sequences, residues, channels), bf16),
            pltpu.VMEM((sequences, residues, channels), bf16),
            pltpu.VMEM((sequences, 2, peers * ROWS, channels), bf16),
            pltpu.VMEM((HEADS, peers * ROWS, residues), f32),
            pltpu.VMEM(block, bf16),
            pltpu.VMEM(block, bf16),
            pltpu.VMEM((2, everyone * ROWS, 128), f32),
            pltpu.VMEM((2, everyone * ROWS, 128), f32),
            pltpu.VMEM((2, everyone * ROWS, 128), f32),
            pltpu.VMEM((everyone * ROWS, channels), bf16),
            pltpu.VMEM((GROUP, everyone, 128), bf16),
            pltpu.VMEM((everyone * ROWS, channels), f32),
            pltpu.SemaphoreType.DMA,
            pltpu.SemaphoreType.DMA((count,)),
            pltpu.SemaphoreType.DMA((2, 2, peers)),
            pltpu.SemaphoreType.DMA((2, peers, pairs // PIECE)),
            pltpu.SemaphoreType.DMA((2, peers, pairs // PIECE)),
        ],
        compiler_params=pltpu.CompilerParams(
            vmem_limit_bytes=VMEM_LIMIT, collective_id=0, has_side_effects=True
        ),
        name="both_attentions",
    )(pair_state, pair_weight, state, tokens, residue_mask, sequence_mask, table, *weights)


def body(
    alignment_state,
    token_index_grid,
    sequence_mask,
    residue_mask,
    pair_state,
    token_embedding_table,
    pair_bias_weight,
    row_query_weight,
    row_key_weight,
    row_value_weight,
    row_gate_weight,
    row_output_weight,
    column_query_weight,
    column_key_weight,
    column_value_weight,
    column_gate_weight,
    column_output_weight,
):
    return both_attentions(
        pair_state, pair_bias_weight.T, alignment_state, token_index_grid, residue_mask[None, :],
        sequence_mask[None, :], token_embedding_table,
        (row_query_weight, row_key_weight, row_value_weight, row_gate_weight, row_output_weight,
         column_query_weight, column_key_weight, column_value_weight, column_gate_weight,
         column_output_weight),
    )


def solution(mesh):
    split = P(("dp", "dap"), None, None)
    in_specs = (
        split, P(("dp", "dap"), None), P("dp"), P("dp"), split,
    ) + (P(),) * 12
    return jax.shard_map(
        body, mesh=mesh, in_specs=in_specs, out_specs=P("dp", "dap", None), check_vma=False
    )
```

```python
import functools

import jax
import jax.numpy as jnp
from jax import lax
from jax.experimental import pallas as pl
from jax.experimental.pallas import tpu as pltpu
from jax.sharding import PartitionSpec as P

HEADS = 8
HEAD_DIM = 32
GROUP = 4
TOKEN_KINDS = 23
EPSILON = 1e-05
LOG2E = 1.4426950408889634
MASKED = -1e9
ROWS = 8
PIECE = 2
COLUMNS = 2
LATER = 2.5
PROJECT_STEPS = (0, 6, 10, 10, 10, 10, 10, 12)
ATTEND_STEPS = (20, 20, 22, 0)
XS, ZS, YS = 4, 2, 4
MESH = pl.DeviceIdType.MESH
VMEM_LIMIT = 60 * 1024 * 1024

NT = (((1,), (1,)), ((), ()))
TN = (((0,), (0,)), ((), ()))


def dot(a, b, dims=(((1,), (0,)), ((), ()))):
    return lax.dot_general(a, b, dims, preferred_element_type=jnp.float32)


def normalize(values):
    centered = values - jnp.mean(values, axis=-1, keepdims=True)
    variance = jnp.mean(centered * centered, axis=-1, keepdims=True)
    return centered * lax.rsqrt(variance + EPSILON)


def sigmoid(x):
    return 0.5 * jnp.tanh(0.5 * x) + 0.5


def lane_head(shape):
    return lax.broadcasted_iota(jnp.int32, shape, len(shape) - 1) // HEAD_DIM


def head_lanes(inner):
    return (lane_head((1, 128)) == inner).astype(jnp.float32).astype(jnp.bfloat16)


def attend(queries, key_at, value_at, ones_at, bias_at):
    halves = []
    for group in range(HEADS // GROUP):
        q = queries[:, 128 * group:128 * (group + 1)]
        keyed, valued = key_at(group), value_at(group)
        all_probs, all_values = [], []
        for inner in range(GROUP):
            mine = head_lanes(inner)
            scores = dot(q, keyed * mine, NT)
            if bias_at is not None:
                scores = scores + bias_at(group * GROUP + inner)
            top = jnp.max(scores, axis=-1, keepdims=True)
            all_probs.append(jnp.exp2(scores - top).astype(jnp.bfloat16))
            all_values.append(jnp.concatenate([valued * mine, ones_at(inner)], axis=1))
        total = dot(jnp.concatenate(all_probs, axis=1), jnp.concatenate(all_values, axis=0))
        halves.append(total[:, 0:128] / total[:, 128:256])
    return jnp.concatenate(halves, axis=1)


def gather_plan():
    def place(half, u, z, v):
        return (v % XS, z % ZS, u % YS) if half == 0 else (u % XS, z % ZS, v % YS)

    first, steps = [], []
    for rows in range(2):
        for half in range(2):
            part = (rows, half)
            for target in ((1, 0, 0), (-1, 0, 0), (2, 0, 0), (0, 1, 0), (0, 0, 1), (0, 0, -1), (0, 0, 2)):
                first.append((part, (0, 0, 0), place(half, *target)))
            for u in (0, 1, -1, 2):
                for z in range(2):
                    for v in (0, 1, -1, 2):
                        if (u, z, v) == (0, 0, 0):
                            continue
                        to = []
                        if v == 0 and z == 0:
                            to.append((0, 1, 0))
                        if v == 0:
                            to += [(0, 0, 1), (0, 0, -1), (0, 0, 2)]
                        hops = abs(u) + abs(v) + 1.5 * z
                        order = hops + LATER * rows + (0 if to else 0.75)
                        steps.append((order, part, place(half, u, z, v), [place(half, *t) for t in to]))
    steps.sort(key=lambda step: step[:3])
    return first, [step[1:] for step in steps]


def fill_slots(steps):
    slots, place = {}, 0
    room = [("project", s, n) for s, n in enumerate(PROJECT_STEPS)]
    room += [("attend", s, n) for s, n in enumerate(ATTEND_STEPS)]
    for stage, s, count in room:
        slots[stage, s] = steps[place:place + count]
        place += count
    rest = steps[place:]
    early = []
    for (stage, s), taken in slots.items():
        if stage == "attend":
            early += [step for step in taken if step[0][0] == 0]
            slots[stage, s] = [step for step in taken if step[0][0] == 1]
    early += [step for step in rest if step[0][0] == 0]
    return slots, early, [step for step in rest if step[0][0] == 1]


def kernel(
    pair_ref, pair_weight_ref, state_ref, token_ref, residue_mask_ref, sequence_mask_ref, table_ref,
    row_wq, row_wk, row_wv, row_wg, row_wo, col_wq, col_wk, col_wv, col_wg, col_wo,
    out_ref,
    local_ref, bias_ref, embedded_ref, query_ref, key_ref, value_ref, gate_ref, wide_ref,
    updated_ref, arrived_ref, col_query, col_key, col_value, col_gate, live_ref, result_ref,
    local_sem, gather_send, gather_recv, turn_send, turn_recv,
):
    sequences, residues, channels = local_ref.shape
    rows_each, _, pair_channels = pair_ref.shape
    peers = residues // rows_each
    me = lax.axis_index("dap")
    x, z, y = me // (ZS * YS), (me // YS) % ZS, me % YS

    def at(offset):
        dx, dz, dy = offset
        return (((x + dx) % XS) * ZS + (z + dz) % ZS) * YS + (y + dy) % YS

    load = pltpu.make_async_copy(state_ref, local_ref, local_sem)
    load.start()
    barrier = pltpu.get_barrier_semaphore()
    for step in range(1, peers):
        pl.semaphore_signal(
            barrier, inc=1, device_id={"dap": (me + step) % peers}, device_id_type=MESH
        )

    first, steps = gather_plan()
    sends = first + [(part, block, target) for part, block, to in steps for target in to]
    number = {send: i for i, send in enumerate(sends)}

    def gather_copy(part, block, target, index):
        rows, half = part
        piece = bias_ref.at[rows, block, pl.ds(half * (HEADS // 2) * ROWS, HEADS // 2 * ROWS)]
        return pltpu.make_async_remote_copy(
            src_ref=piece, dst_ref=piece,
            send_sem=gather_send.at[index], recv_sem=gather_recv.at[rows, half, block],
            device_id={"dap": target}, device_id_type=MESH,
        )

    def start(send):
        part, block, target = send
        gather_copy(part, at(block), at(target), number[send]).start()

    def run(steps):
        for part, block, to in steps:
            gather_copy(part, at(block), at((0, 1, 0)), 0).wait_recv()
            for target in to:
                start((part, block, target))

    averaging = jnp.full((pair_channels, pair_channels), 1.0 / pair_channels, jnp.bfloat16)
    spread = pair_weight_ref[...].astype(jnp.float32)
    spread = jnp.broadcast_to(spread[:, None, :], (HEADS, ROWS, pair_channels))
    spread = spread.reshape(HEADS * ROWS, pair_channels)
    row_of = lax.broadcasted_iota(jnp.int32, spread.shape, 0) % ROWS
    for rows in range(2):
        total = None
        for row in range(ROWS):
            block = pair_ref[rows * ROWS + row]
            centered = block.astype(jnp.float32) - dot(block, averaging)
            variance = dot((centered * centered).astype(jnp.bfloat16), averaging)
            normed = (centered * lax.rsqrt(variance + EPSILON)).astype(jnp.bfloat16)
            weight = jnp.where(row_of == row, spread, 0.0).astype(jnp.bfloat16)
            product = dot(weight, normed, NT)
            total = product if total is None else total + product
        bias_ref[rows, me] = total.astype(jnp.bfloat16)
        if rows == 0:
            pl.semaphore_wait(barrier, peers - 1)
        for send in first:
            if send[0][0] == rows:
                start(send)

    slots, early, rest = fill_slots(steps)
    load.wait()

    def by_half(values):
        return jnp.swapaxes(values.reshape(peers, 2, ROWS, channels), 0, 1).reshape(
            2, peers * ROWS, channels
        )

    @pl.loop(0, sequences)
    def _(s):
        tokens = token_ref[pl.ds(s, 1), :]
        kinds = lax.broadcasted_iota(jnp.int32, (TOKEN_KINDS, residues), 0)
        indicator = (kinds == tokens).astype(jnp.float32).astype(jnp.bfloat16)
        embedded = local_ref[s].astype(jnp.float32) + dot(indicator, table_ref[...], TN)
        embedded_ref[s] = by_half(embedded)
        normed = normalize(embedded).astype(jnp.bfloat16)
        queries = dot(normed, row_wq[...]) * (HEAD_DIM ** -0.5 * LOG2E)
        query_ref[s] = by_half(queries).astype(jnp.bfloat16)
        key_ref[s] = dot(normed, row_wk[...]).astype(jnp.bfloat16)
        value_ref[s] = dot(normed, row_wv[...]).astype(jnp.bfloat16)
        gate_ref[s] = by_half(sigmoid(dot(normed, row_wg[...]))).astype(jnp.bfloat16)
        for k in range(sequences):
            if slots["project", k]:
                pl.when(s == k)(functools.partial(run, slots["project", k]))

    real = residue_mask_ref[...] > 0
    pairs = sequences // 2
    pieces = pairs // PIECE

    def turn_copy(rows, target, slot, piece):
        span = pl.ds(piece * PIECE, PIECE)
        return pltpu.make_async_remote_copy(
            src_ref=updated_ref.at[rows, target, span], dst_ref=arrived_ref.at[rows, slot, span],
            send_sem=turn_send.at[rows, target, piece], recv_sem=turn_recv.at[rows, slot, piece],
            device_id={"dap": target}, device_id_type=MESH,
        )

    run(early)

    @pl.loop(0, 2)
    def _(rows):
        if rest:
            pl.when(rows == 1)(functools.partial(run, rest))
        for head in range(0, HEADS, 2):
            both = bias_ref[rows, :, ROWS * head:ROWS * (head + 2), :].astype(jnp.float32) * LOG2E
            for i in range(2):
                part = both[:, ROWS * i:ROWS * (i + 1), :].reshape(peers * ROWS, residues)
                wide_ref[head + i] = jnp.where(real, part, MASKED)

        @pl.loop(0, pairs)
        def _(p):
            results = []
            for i in range(2):
                s = 2 * p + i
                attended = attend(
                    query_ref[s, rows],
                    lambda g: key_ref[s, :, 128 * g:128 * (g + 1)],
                    lambda g: value_ref[s, :, 128 * g:128 * (g + 1)],
                    lambda inner: jnp.broadcast_to(head_lanes(inner), (residues, 128)),
                    lambda head: wide_ref[head],
                )
                mixed = (attended * gate_ref[s, rows].astype(jnp.float32)).astype(jnp.bfloat16)
                updated = embedded_ref[s, rows] + dot(mixed, row_wo[...])
                results.append(updated.reshape(peers, ROWS, channels))
            updated_ref[rows, :, p] = jnp.concatenate(results, axis=1).astype(jnp.bfloat16)
            arrived_ref[rows, me, p] = updated_ref[rows, me, p]
            for k in range(pairs):
                if slots["attend", k]:
                    pl.when((rows == 0) & (p == k))(functools.partial(run, slots["attend", k]))

            @pl.when(p % PIECE == PIECE - 1)
            def _():
                for step in range(1, peers):
                    turn_copy(rows, (me + step) % peers, me, p // PIECE).start()

    tokens = 512
    lines = tokens // ROWS
    sources = lines // sequences
    everyone = peers * sequences
    real = jnp.broadcast_to(sequence_mask_ref[...].astype(jnp.float32), (128, everyone))
    real = jnp.transpose(real)
    for inner in range(GROUP):
        live_ref[inner] = real.astype(jnp.bfloat16) * head_lanes(inner)
    real = jnp.concatenate([real, real], axis=1)

    for rows in range(2):
        def arrivals(i):
            part = arrived_ref[rows, pl.ds(i * sources, sources)]
            return part.astype(jnp.float32).reshape(tokens, channels)

        def span_of(i):
            return pl.ds(pl.multiple_of(i * tokens, tokens), tokens)

        @pl.loop(0, peers // sources)
        def _(i):
            for j in range(sources):
                source = i * sources + j

                @pl.when(source != me)
                def _():
                    for piece in range(pieces):
                        turn_copy(rows, source, source, piece).wait_recv()
            span = span_of(i)
            normed = normalize(arrivals(i)).astype(jnp.bfloat16)
            queries = dot(normed, col_wq[...]) * (HEAD_DIM ** -0.5 * LOG2E)
            keyed = dot(normed, col_wk[...])
            valued = dot(normed, col_wv[...])
            for half in range(2):
                lanes = slice(128 * half, 128 * (half + 1))
                col_query[half, span, :] = queries[:, lanes]
                col_key[half, span, :] = keyed[:, lanes]
                col_value[half, span, :] = valued[:, lanes]
            col_gate[span, :] = sigmoid(dot(normed, col_wg[...])).astype(jnp.bfloat16)

        @pl.loop(0, ROWS // COLUMNS)
        def _(i):
            spans = [pl.ds(i * COLUMNS + j, everyone, stride=ROWS) for j in range(COLUMNS)]

            def line(ref, span):
                return jnp.concatenate([ref[half, span, :] for half in range(2)], axis=1)

            loaded = [[line(ref, span) for ref in (col_query, col_key, col_value)] for span in spans]
            results = []
            for queries, keyed, valued in loaded:
                keyed = jnp.where(real > 0.0, keyed, keyed[0:1, :]).astype(jnp.bfloat16)
                valued = (valued * real).astype(jnp.bfloat16)
                results.append(attend(
                    queries.astype(jnp.bfloat16),
                    lambda g: keyed[:, 128 * g:128 * (g + 1)],
                    lambda g: valued[:, 128 * g:128 * (g + 1)],
                    lambda inner: live_ref[inner],
                    None,
                ))
            for span, attended in zip(spans, results):
                for half in range(2):
                    col_query[half, span, :] = attended[:, 128 * half:128 * (half + 1)]

        @pl.loop(0, peers // sources)
        def _(i):
            span = span_of(i)
            attended = jnp.concatenate([col_query[half, span, :] for half in range(2)], axis=1)
            mixed = (attended * col_gate[span, :].astype(jnp.float32)).astype(jnp.bfloat16)
            result = arrivals(i) + dot(mixed, col_wo[...])
            if rows == 0:
                result_ref[span, :] = result
            else:
                both = [result_ref[span, :], result]
                both = [part.reshape(lines, ROWS, channels) for part in both]
                out_ref[pl.ds(pl.multiple_of(i * lines, lines), lines)] = (
                    jnp.concatenate(both, axis=1).astype(jnp.bfloat16)
                )

    for send in sends:
        part, block, target = send
        gather_copy(part, at(block), at(target), number[send]).wait_send()

    @pl.loop(1, peers)
    def _(step):
        for rows in range(2):
            for piece in range(pieces):
                turn_copy(rows, (me + step) % peers, me, piece).wait_send()


def both_attentions(pair_state, pair_weight, state, tokens, residue_mask, sequence_mask, table, weights):
    sequences, residues, channels = state.shape
    rows_each = pair_state.shape[0]
    peers = residues // rows_each
    everyone = peers * sequences
    pairs = sequences // 2
    block = (2, peers, pairs, 2 * ROWS, channels)
    first, steps = gather_plan()
    count = len(first) + sum(len(step[2]) for step in steps)
    whole = pl.BlockSpec(memory_space=pltpu.VMEM)
    bf16, f32 = jnp.bfloat16, jnp.float32
    return pl.pallas_call(
        kernel,
        out_shape=jax.ShapeDtypeStruct((everyone, rows_each, channels), bf16),
        in_specs=[whole] * 2 + [pl.BlockSpec(memory_space=pl.ANY)] + [whole] * 14,
        out_specs=whole,
        scratch_shapes=[
            pltpu.VMEM((sequences, residues, channels), bf16),
            pltpu.VMEM((2, peers, HEADS * ROWS, residues), bf16),
            pltpu.VMEM((sequences, 2, peers * ROWS, channels), f32),
            pltpu.VMEM((sequences, 2, peers * ROWS, channels), bf16),
            pltpu.VMEM((sequences, residues, channels), bf16),
            pltpu.VMEM((sequences, residues, channels), bf16),
            pltpu.VMEM((sequences, 2, peers * ROWS, channels), bf16),
            pltpu.VMEM((HEADS, peers * ROWS, residues), f32),
            pltpu.VMEM(block, bf16),
            pltpu.VMEM(block, bf16),
            pltpu.VMEM((2, everyone * ROWS, 128), f32),
            pltpu.VMEM((2, everyone * ROWS, 128), f32),
            pltpu.VMEM((2, everyone * ROWS, 128), f32),
            pltpu.VMEM((everyone * ROWS, channels), bf16),
            pltpu.VMEM((GROUP, everyone, 128), bf16),
            pltpu.VMEM((everyone * ROWS, channels), f32),
            pltpu.SemaphoreType.DMA,
            pltpu.SemaphoreType.DMA((count,)),
            pltpu.SemaphoreType.DMA((2, 2, peers)),
            pltpu.SemaphoreType.DMA((2, peers, pairs // PIECE)),
            pltpu.SemaphoreType.DMA((2, peers, pairs // PIECE)),
        ],
        compiler_params=pltpu.CompilerParams(
            vmem_limit_bytes=VMEM_LIMIT, collective_id=0, has_side_effects=True
        ),
        name="both_attentions",
    )(pair_state, pair_weight, state, tokens, residue_mask, sequence_mask, table, *weights)


def body(
    alignment_state,
    token_index_grid,
    sequence_mask,
    residue_mask,
    pair_state,
    token_embedding_table,
    pair_bias_weight,
    row_query_weight,
    row_key_weight,
    row_value_weight,
    row_gate_weight,
    row_output_weight,
    column_query_weight,
    column_key_weight,
    column_value_weight,
    column_gate_weight,
    column_output_weight,
):
    return both_attentions(
        pair_state, pair_bias_weight.T, alignment_state, token_index_grid, residue_mask[None, :],
        sequence_mask[None, :], token_embedding_table,
        (row_query_weight, row_key_weight, row_value_weight, row_gate_weight, row_output_weight,
         column_query_weight, column_key_weight, column_value_weight, column_gate_weight,
         column_output_weight),
    )


def solution(mesh):
    split = P(("dp", "dap"), None, None)
    in_specs = (
        split, P(("dp", "dap"), None), P("dp"), P("dp"), split,
    ) + (P(),) * 12
    return jax.shard_map(
        body, mesh=mesh, in_specs=in_specs, out_specs=P("dp", "dap", None), check_vma=False
    )
```

```python
import functools

import jax
import jax.numpy as jnp
from jax import lax
from jax.experimental import pallas as pl
from jax.experimental.pallas import tpu as pltpu
from jax.sharding import PartitionSpec as P

HEADS = 8
HEAD_DIM = 32
GROUP = 4
TOKEN_KINDS = 23
EPSILON = 1e-05
LOG2E = 1.4426950408889634
MASKED = -1e9
ROWS = 8
PIECE = 2
COLUMNS = 4
RELAY_AFTER = (((0, 1), 1), ((1, 0), 4), ((1, 1), 6))
XS, ZS, YS = 4, 2, 4
MESH = pl.DeviceIdType.MESH
VMEM_LIMIT = 60 * 1024 * 1024

NT = (((1,), (1,)), ((), ()))
TN = (((0,), (0,)), ((), ()))


def dot(a, b, dims=(((1,), (0,)), ((), ()))):
    return lax.dot_general(a, b, dims, preferred_element_type=jnp.float32)


def normalize(values):
    centered = values - jnp.mean(values, axis=-1, keepdims=True)
    variance = jnp.mean(centered * centered, axis=-1, keepdims=True)
    return centered * lax.rsqrt(variance + EPSILON)


def sigmoid(x):
    return 0.5 * jnp.tanh(0.5 * x) + 0.5


def lane_head(shape):
    return lax.broadcasted_iota(jnp.int32, shape, len(shape) - 1) // HEAD_DIM


def head_lanes(inner):
    return (lane_head((1, 128)) == inner).astype(jnp.float32).astype(jnp.bfloat16)


def attend(queries, key_at, value_at, ones_at, bias_at):
    halves = []
    for group in range(HEADS // GROUP):
        q = queries[:, 128 * group:128 * (group + 1)]
        keyed, valued = key_at(group), value_at(group)
        all_probs, all_values = [], []
        for inner in range(GROUP):
            mine = head_lanes(inner)
            scores = dot(q, keyed * mine, NT)
            if bias_at is not None:
                scores = scores + bias_at(group * GROUP + inner)
            top = jnp.max(scores, axis=-1, keepdims=True)
            all_probs.append(jnp.exp2(scores - top).astype(jnp.bfloat16))
            all_values.append(jnp.concatenate([valued * mine, ones_at(inner)], axis=1))
        total = dot(jnp.concatenate(all_probs, axis=1), jnp.concatenate(all_values, axis=0))
        halves.append(total[:, 0:128] / total[:, 128:256])
    return jnp.concatenate(halves, axis=1)


def gather_plan():
    def place(half, u, z, v):
        return (v % XS, z % ZS, u % YS) if half == 0 else (u % XS, z % ZS, v % YS)

    first, steps = [], []
    for rows in range(2):
        for half in range(2):
            part = (rows, half)
            for target in ((1, 0, 0), (-1, 0, 0), (2, 0, 0), (0, 1, 0), (0, 0, 1), (0, 0, -1), (0, 0, 2)):
                first.append((part, (0, 0, 0), place(half, *target)))
            for u in (0, 1, -1, 2):
                for z in range(2):
                    for v in (0, 1, -1, 2):
                        if (u, z, v) == (0, 0, 0):
                            continue
                        to = []
                        if v == 0 and z == 0:
                            to.append((0, 1, 0))
                        if v == 0:
                            to += [(0, 0, 1), (0, 0, -1), (0, 0, 2)]
                        hops = abs(u) + abs(v) + 1.5 * z
                        order = hops
                        steps.append((order, part, place(half, u, z, v), [place(half, *t) for t in to]))
    steps.sort(key=lambda step: step[:3])
    return first, [step[1:] for step in steps]


def split_steps(steps):
    relays = {(rows, level): [] for rows in range(2) for level in range(2)}
    waits = ([], [])
    for step in steps:
        (rows, _), block, to = step
        if to:
            relays[rows, block[1]].append(step)
        else:
            waits[rows].append(step)
    return relays, waits


def kernel(
    pair_ref, pair_weight_ref, state_ref, token_ref, residue_mask_ref, sequence_mask_ref, table_ref,
    row_wq, row_wk, row_wv, row_wg, row_wo, col_wq, col_wk, col_wv, col_wg, col_wo,
    out_ref,
    local_ref, bias_ref, embedded_ref, query_ref, key_ref, value_ref, gate_ref, wide_ref,
    updated_ref, arrived_ref, column_ref, live_ref,
    local_sem, gather_send, gather_recv, turn_send, turn_recv,
):
    sequences, residues, channels = local_ref.shape
    rows_each, _, pair_channels = pair_ref.shape
    peers = residues // rows_each
    me = lax.axis_index("dap")
    x, z, y = me // (ZS * YS), (me // YS) % ZS, me % YS

    def at(offset):
        dx, dz, dy = offset
        return (((x + dx) % XS) * ZS + (z + dz) % ZS) * YS + (y + dy) % YS

    load = pltpu.make_async_copy(state_ref, local_ref, local_sem)
    load.start()
    barrier = pltpu.get_barrier_semaphore()
    for step in range(1, peers):
        pl.semaphore_signal(
            barrier, inc=1, device_id={"dap": (me + step) % peers}, device_id_type=MESH
        )

    first, steps = gather_plan()
    sends = first + [(part, block, target) for part, block, to in steps for target in to]
    number = {send: i for i, send in enumerate(sends)}

    def gather_copy(part, block, target, index):
        rows, half = part
        piece = bias_ref.at[rows, block, pl.ds(half * (HEADS // 2) * ROWS, HEADS // 2 * ROWS)]
        return pltpu.make_async_remote_copy(
            src_ref=piece, dst_ref=piece,
            send_sem=gather_send.at[index], recv_sem=gather_recv.at[rows, half, block],
            device_id={"dap": target}, device_id_type=MESH,
        )

    def start(send):
        part, block, target = send
        gather_copy(part, at(block), at(target), number[send]).start()

    def run(steps):
        for part, block, to in steps:
            gather_copy(part, at(block), at((0, 1, 0)), 0).wait_recv()
            for target in to:
                start((part, block, target))

    averaging = jnp.full((pair_channels, pair_channels), 1.0 / pair_channels, jnp.bfloat16)
    spread = pair_weight_ref[...].astype(jnp.float32)
    spread = jnp.broadcast_to(spread[:, None, :], (HEADS, ROWS, pair_channels))
    spread = spread.reshape(HEADS * ROWS, pair_channels)
    row_of = lax.broadcasted_iota(jnp.int32, spread.shape, 0) % ROWS
    for rows in range(2):
        total = None
        for row in range(ROWS):
            block = pair_ref[rows * ROWS + row]
            centered = block.astype(jnp.float32) - dot(block, averaging)
            variance = dot((centered * centered).astype(jnp.bfloat16), averaging)
            normed = (centered * lax.rsqrt(variance + EPSILON)).astype(jnp.bfloat16)
            weight = jnp.where(row_of == row, spread, 0.0).astype(jnp.bfloat16)
            product = dot(weight, normed, NT)
            total = product if total is None else total + product
        bias_ref[rows, me] = total.astype(jnp.bfloat16)
        if rows == 0:
            pl.semaphore_wait(barrier, peers - 1)
        for send in first:
            if send[0][0] == rows:
                start(send)

    relays, waits = split_steps(steps)
    run(relays[0, 0])
    load.wait()

    def by_half(values):
        return jnp.swapaxes(values.reshape(peers, 2, ROWS, channels), 0, 1).reshape(
            2, peers * ROWS, channels
        )

    @pl.loop(0, sequences)
    def _(s):
        tokens = token_ref[pl.ds(s, 1), :]
        kinds = lax.broadcasted_iota(jnp.int32, (TOKEN_KINDS, residues), 0)
        indicator = (kinds == tokens).astype(jnp.float32).astype(jnp.bfloat16)
        embedded = local_ref[s].astype(jnp.float32) + dot(indicator, table_ref[...], TN)
        embedded_ref[s] = by_half(embedded)
        normed = normalize(embedded).astype(jnp.bfloat16)
        queries = dot(normed, row_wq[...]) * (HEAD_DIM ** -0.5 * LOG2E)
        query_ref[s] = by_half(queries).astype(jnp.bfloat16)
        key_ref[s] = dot(normed, row_wk[...]).astype(jnp.bfloat16)
        value_ref[s] = dot(normed, row_wv[...]).astype(jnp.bfloat16)
        gate_ref[s] = by_half(sigmoid(dot(normed, row_wg[...]))).astype(jnp.bfloat16)
        for which, k in RELAY_AFTER:
            pl.when(s == k)(functools.partial(run, relays[which]))

    real = residue_mask_ref[...] > 0
    pairs = sequences // 2
    pieces = pairs // PIECE

    def turn_copy(rows, target, slot, piece):
        span = pl.ds(piece * PIECE, PIECE)
        return pltpu.make_async_remote_copy(
            src_ref=updated_ref.at[rows, target, span], dst_ref=arrived_ref.at[rows, slot, span],
            send_sem=turn_send.at[rows, target, piece], recv_sem=turn_recv.at[rows, slot, piece],
            device_id={"dap": target}, device_id_type=MESH,
        )

    run(waits[0])

    @pl.loop(0, 2)
    def _(rows):
        pl.when(rows == 1)(functools.partial(run, waits[1]))

        for head in range(0, HEADS, 2):
            both = bias_ref[rows, :, ROWS * head:ROWS * (head + 2), :].astype(jnp.float32) * LOG2E
            for i in range(2):
                part = both[:, ROWS * i:ROWS * (i + 1), :].reshape(peers * ROWS, residues)
                wide_ref[head + i] = jnp.where(real, part, MASKED)

        @pl.loop(0, pairs)
        def _(p):
            results = []
            for i in range(2):
                s = 2 * p + i
                attended = attend(
                    query_ref[s, rows],
                    lambda g: key_ref[s, :, 128 * g:128 * (g + 1)],
                    lambda g: value_ref[s, :, 128 * g:128 * (g + 1)],
                    lambda inner: jnp.broadcast_to(head_lanes(inner), (residues, 128)),
                    lambda head: wide_ref[head],
                )
                mixed = (attended * gate_ref[s, rows].astype(jnp.float32)).astype(jnp.bfloat16)
                updated = embedded_ref[s, rows] + dot(mixed, row_wo[...])
                results.append(updated.reshape(peers, ROWS, channels))
            updated_ref[rows, :, p] = jnp.concatenate(results, axis=1).astype(jnp.bfloat16)
            arrived_ref[rows, me, p] = updated_ref[rows, me, p]

            @pl.when(p % PIECE == PIECE - 1)
            def _():
                for step in range(1, peers):
                    turn_copy(rows, (me + step) % peers, me, p // PIECE).start()

    tokens = 512
    lines = tokens // ROWS
    sources = lines // sequences
    everyone = peers * sequences
    real = jnp.broadcast_to(sequence_mask_ref[...].astype(jnp.float32), (128, everyone))
    real = jnp.transpose(real)
    for inner in range(GROUP):
        live_ref[inner] = real.astype(jnp.bfloat16) * head_lanes(inner)
    real = jnp.concatenate([real, real], axis=1)

    def span_of(i):
        return pl.ds(pl.multiple_of(i * tokens, tokens), tokens)

    for rows in range(2):
        @pl.loop(0, peers // sources)
        def _(i):
            for j in range(sources):
                source = i * sources + j

                @pl.when(source != me)
                def _():
                    for piece in range(pieces):
                        turn_copy(rows, source, source, piece).wait_recv()
            part = arrived_ref[rows, pl.ds(i * sources, sources)]
            part = part.astype(jnp.float32).reshape(tokens, channels)
            for half in range(2):
                column_ref[rows, half, span_of(i), :] = part[:, 128 * half:128 * (half + 1)]

        @pl.loop(0, ROWS // COLUMNS)
        def _(i):
            spans = [pl.ds(i * COLUMNS + j, everyone, stride=ROWS) for j in range(COLUMNS)]
            updated = jnp.concatenate([
                jnp.concatenate([column_ref[rows, half, span, :] for half in range(2)], axis=1)
                for span in spans
            ], axis=0)
            normed = normalize(updated).astype(jnp.bfloat16)
            queries = dot(normed, col_wq[...]) * (HEAD_DIM ** -0.5 * LOG2E)
            queries = queries.astype(jnp.bfloat16)
            all_keyed = dot(normed, col_wk[...])
            all_valued = dot(normed, col_wv[...])
            gate = sigmoid(dot(normed, col_wg[...]))
            results = []
            for j in range(COLUMNS):
                mine = slice(everyone * j, everyone * (j + 1))
                keyed = all_keyed[mine]
                keyed = jnp.where(real > 0.0, keyed, keyed[0:1, :]).astype(jnp.bfloat16)
                valued = (all_valued[mine] * real).astype(jnp.bfloat16)
                results.append(attend(
                    queries[mine],
                    lambda g: keyed[:, 128 * g:128 * (g + 1)],
                    lambda g: valued[:, 128 * g:128 * (g + 1)],
                    lambda inner: live_ref[inner],
                    None,
                ))
            mixed = (jnp.concatenate(results, axis=0) * gate).astype(jnp.bfloat16)
            result = updated + dot(mixed, col_wo[...])
            for j, span in enumerate(spans):
                mine = slice(everyone * j, everyone * (j + 1))
                for half in range(2):
                    column_ref[rows, half, span, :] = result[mine, 128 * half:128 * (half + 1)]

    @pl.loop(0, peers // sources)
    def _(i):
        both = []
        for rows in range(2):
            halves = [column_ref[rows, half, span_of(i), :] for half in range(2)]
            both.append(jnp.concatenate(halves, axis=1).reshape(lines, ROWS, channels))
        out_ref[pl.ds(pl.multiple_of(i * lines, lines), lines)] = (
            jnp.concatenate(both, axis=1).astype(jnp.bfloat16)
        )

    for send in sends:
        part, block, target = send
        gather_copy(part, at(block), at(target), number[send]).wait_send()

    @pl.loop(1, peers)
    def _(step):
        for rows in range(2):
            for piece in range(pieces):
                turn_copy(rows, (me + step) % peers, me, piece).wait_send()


def both_attentions(pair_state, pair_weight, state, tokens, residue_mask, sequence_mask, table, weights):
    sequences, residues, channels = state.shape
    rows_each = pair_state.shape[0]
    peers = residues // rows_each
    everyone = peers * sequences
    pairs = sequences // 2
    block = (2, peers, pairs, 2 * ROWS, channels)
    first, steps = gather_plan()
    count = len(first) + sum(len(step[2]) for step in steps)
    whole = pl.BlockSpec(memory_space=pltpu.VMEM)
    bf16, f32 = jnp.bfloat16, jnp.float32
    return pl.pallas_call(
        kernel,
        out_shape=jax.ShapeDtypeStruct((everyone, rows_each, channels), bf16),
        in_specs=[whole] * 2 + [pl.BlockSpec(memory_space=pl.ANY)] + [whole] * 14,
        out_specs=whole,
        scratch_shapes=[
            pltpu.VMEM((sequences, residues, channels), bf16),
            pltpu.VMEM((2, peers, HEADS * ROWS, residues), bf16),
            pltpu.VMEM((sequences, 2, peers * ROWS, channels), f32),
            pltpu.VMEM((sequences, 2, peers * ROWS, channels), bf16),
            pltpu.VMEM((sequences, residues, channels), bf16),
            pltpu.VMEM((sequences, residues, channels), bf16),
            pltpu.VMEM((sequences, 2, peers * ROWS, channels), bf16),
            pltpu.VMEM((HEADS, peers * ROWS, residues), f32),
            pltpu.VMEM(block, bf16),
            pltpu.VMEM(block, bf16),
            pltpu.VMEM((2, 2, everyone * ROWS, 128), f32),
            pltpu.VMEM((GROUP, everyone, 128), bf16),
            pltpu.SemaphoreType.DMA,
            pltpu.SemaphoreType.DMA((count,)),
            pltpu.SemaphoreType.DMA((2, 2, peers)),
            pltpu.SemaphoreType.DMA((2, peers, pairs // PIECE)),
            pltpu.SemaphoreType.DMA((2, peers, pairs // PIECE)),
        ],
        compiler_params=pltpu.CompilerParams(
            vmem_limit_bytes=VMEM_LIMIT, collective_id=0, has_side_effects=True
        ),
        name="both_attentions",
    )(pair_state, pair_weight, state, tokens, residue_mask, sequence_mask, table, *weights)


def body(
    alignment_state,
    token_index_grid,
    sequence_mask,
    residue_mask,
    pair_state,
    token_embedding_table,
    pair_bias_weight,
    row_query_weight,
    row_key_weight,
    row_value_weight,
    row_gate_weight,
    row_output_weight,
    column_query_weight,
    column_key_weight,
    column_value_weight,
    column_gate_weight,
    column_output_weight,
):
    return both_attentions(
        pair_state, pair_bias_weight.T, alignment_state, token_index_grid, residue_mask[None, :],
        sequence_mask[None, :], token_embedding_table,
        (row_query_weight, row_key_weight, row_value_weight, row_gate_weight, row_output_weight,
         column_query_weight, column_key_weight, column_value_weight, column_gate_weight,
         column_output_weight),
    )


def solution(mesh):
    split = P(("dp", "dap"), None, None)
    in_specs = (
        split, P(("dp", "dap"), None), P("dp"), P("dp"), split,
    ) + (P(),) * 12
    return jax.shard_map(
        body, mesh=mesh, in_specs=in_specs, out_specs=P("dp", "dap", None), check_vma=False
    )
```

```python
import functools

import jax
import jax.numpy as jnp
from jax import lax
from jax.experimental import pallas as pl
from jax.experimental.pallas import tpu as pltpu
from jax.sharding import PartitionSpec as P

HEADS = 8
HEAD_DIM = 32
GROUP = 4
TOKEN_KINDS = 23
EPSILON = 1e-05
LOG2E = 1.4426950408889634
MASKED = -1e9
ROWS = 8
PIECE = 2
WEIGHTS = 10
COLUMNS = 4
RELAY_AFTER = (((0, 1), 1), ((1, 0), 4), ((1, 1), 6))
XS, ZS, YS = 4, 2, 4
MESH = pl.DeviceIdType.MESH
VMEM_LIMIT = 60 * 1024 * 1024

NT = (((1,), (1,)), ((), ()))
TN = (((0,), (0,)), ((), ()))


def dot(a, b, dims=(((1,), (0,)), ((), ()))):
    return lax.dot_general(a, b, dims, preferred_element_type=jnp.float32)


def normalize(values):
    centered = values - jnp.mean(values, axis=-1, keepdims=True)
    variance = jnp.mean(centered * centered, axis=-1, keepdims=True)
    return centered * lax.rsqrt(variance + EPSILON)


def sigmoid(x):
    return 0.5 * jnp.tanh(0.5 * x) + 0.5


def lane_head(shape):
    return lax.broadcasted_iota(jnp.int32, shape, len(shape) - 1) // HEAD_DIM


def head_lanes(inner):
    return (lane_head((1, 128)) == inner).astype(jnp.float32).astype(jnp.bfloat16)


def attend(queries, key_at, value_at, ones_at, bias_at):
    halves = []
    for group in range(HEADS // GROUP):
        q = queries[:, 128 * group:128 * (group + 1)]
        keyed, valued = key_at(group), value_at(group)
        all_probs, all_values = [], []
        for inner in range(GROUP):
            mine = head_lanes(inner)
            scores = dot(q, keyed * mine, NT)
            if bias_at is not None:
                scores = scores + bias_at(group * GROUP + inner)
            top = jnp.max(scores, axis=-1, keepdims=True)
            all_probs.append(jnp.exp2(scores - top).astype(jnp.bfloat16))
            all_values.append(jnp.concatenate([valued * mine, ones_at(inner)], axis=1))
        total = dot(jnp.concatenate(all_probs, axis=1), jnp.concatenate(all_values, axis=0))
        halves.append(total[:, 0:128] / total[:, 128:256])
    return jnp.concatenate(halves, axis=1)


def gather_plan():
    def place(half, u, z, v):
        return (v % XS, z % ZS, u % YS) if half == 0 else (u % XS, z % ZS, v % YS)

    first, steps = [], []
    for rows in range(2):
        for half in range(2):
            part = (rows, half)
            for target in ((1, 0, 0), (-1, 0, 0), (2, 0, 0), (0, 1, 0), (0, 0, 1), (0, 0, -1), (0, 0, 2)):
                first.append((part, (0, 0, 0), place(half, *target)))
            for u in (0, 1, -1, 2):
                for z in range(2):
                    for v in (0, 1, -1, 2):
                        if (u, z, v) == (0, 0, 0):
                            continue
                        to = []
                        if v == 0 and z == 0:
                            to.append((0, 1, 0))
                        if v == 0:
                            to += [(0, 0, 1), (0, 0, -1), (0, 0, 2)]
                        hops = abs(u) + abs(v) + 1.5 * z
                        order = hops
                        steps.append((order, part, place(half, u, z, v), [place(half, *t) for t in to]))
    steps.sort(key=lambda step: step[:3])
    return first, [step[1:] for step in steps]


def split_steps(steps):
    relays = {(rows, level): [] for rows in range(2) for level in range(2)}
    waits = ([], [])
    for step in steps:
        (rows, _), block, to = step
        if to:
            relays[rows, block[1]].append(step)
        else:
            waits[rows].append(step)
    return relays, waits


def kernel(
    pair_hbm, pair_weight_ref, state_ref, token_ref, residue_mask_ref, sequence_mask_ref, table_ref,
    *refs,
):
    weights_hbm, refs = refs[:WEIGHTS], refs[WEIGHTS:]
    (
        out_ref,
        pair_ref, weights_ref, local_ref, bias_ref, embedded_ref, query_ref, key_ref, value_ref, gate_ref, wide_ref,
        updated_ref, arrived_ref, column_ref, live_ref,
        local_sem, gather_send, gather_recv, turn_send, turn_recv,
    ) = refs
    sequences, residues, channels = local_ref.shape
    rows_each, _, pair_channels = pair_ref.shape
    peers = residues // rows_each
    me = lax.axis_index("dap")
    x, z, y = me // (ZS * YS), (me // YS) % ZS, me % YS

    def at(offset):
        dx, dz, dy = offset
        return (((x + dx) % XS) * ZS + (z + dz) % ZS) * YS + (y + dy) % YS

    half_rows = [pl.ds(ROWS * rows, ROWS) for rows in range(2)]
    load_pair = [
        pltpu.make_async_copy(pair_hbm.at[half_rows[i]], pair_ref.at[half_rows[i]], local_sem.at[i])
        for i in range(2)
    ]
    load = pltpu.make_async_copy(state_ref, local_ref, local_sem.at[2])
    load_weights = [
        pltpu.make_async_copy(weights_hbm[i], weights_ref.at[i], local_sem.at[3 + i])
        for i in range(WEIGHTS)
    ]
    for copy in load_pair + [load] + load_weights:
        copy.start()
    row_wq, row_wk, row_wv, row_wg, row_wo = [weights_ref.at[i] for i in range(5)]
    col_wq, col_wk, col_wv, col_wg, col_wo = [weights_ref.at[i] for i in range(5, WEIGHTS)]
    barrier = pltpu.get_barrier_semaphore()
    for step in range(1, peers):
        pl.semaphore_signal(
            barrier, inc=1, device_id={"dap": (me + step) % peers}, device_id_type=MESH
        )

    first, steps = gather_plan()
    sends = first + [(part, block, target) for part, block, to in steps for target in to]
    number = {send: i for i, send in enumerate(sends)}

    def gather_copy(part, block, target, index):
        rows, half = part
        piece = bias_ref.at[rows, block, pl.ds(half * (HEADS // 2) * ROWS, HEADS // 2 * ROWS)]
        return pltpu.make_async_remote_copy(
            src_ref=piece, dst_ref=piece,
            send_sem=gather_send.at[index], recv_sem=gather_recv.at[rows, half, block],
            device_id={"dap": target}, device_id_type=MESH,
        )

    def start(send):
        part, block, target = send
        gather_copy(part, at(block), at(target), number[send]).start()

    def run(steps):
        for part, block, to in steps:
            gather_copy(part, at(block), at((0, 1, 0)), 0).wait_recv()
            for target in to:
                start((part, block, target))

    averaging = jnp.full((pair_channels, pair_channels), 1.0 / pair_channels, jnp.bfloat16)
    spread = pair_weight_ref[...].astype(jnp.float32)
    spread = jnp.broadcast_to(spread[:, None, :], (HEADS, ROWS, pair_channels))
    spread = spread.reshape(HEADS * ROWS, pair_channels)
    row_of = lax.broadcasted_iota(jnp.int32, spread.shape, 0) % ROWS
    for rows in range(2):
        load_pair[rows].wait()
        total = None
        for row in range(ROWS):
            block = pair_ref[rows * ROWS + row]
            centered = block.astype(jnp.float32) - dot(block, averaging)
            variance = dot((centered * centered).astype(jnp.bfloat16), averaging)
            normed = (centered * lax.rsqrt(variance + EPSILON)).astype(jnp.bfloat16)
            weight = jnp.where(row_of == row, spread, 0.0).astype(jnp.bfloat16)
            product = dot(weight, normed, NT)
            total = product if total is None else total + product
        bias_ref[rows, me] = total.astype(jnp.bfloat16)
        if rows == 0:
            pl.semaphore_wait(barrier, peers - 1)
        for send in first:
            if send[0][0] == rows:
                start(send)

    relays, waits = split_steps(steps)
    run(relays[0, 0])
    load.wait()
    for copy in load_weights:
        copy.wait()

    def by_half(values):
        return jnp.swapaxes(values.reshape(peers, 2, ROWS, channels), 0, 1).reshape(
            2, peers * ROWS, channels
        )

    @pl.loop(0, sequences)
    def _(s):
        tokens = token_ref[pl.ds(s, 1), :]
        kinds = lax.broadcasted_iota(jnp.int32, (TOKEN_KINDS, residues), 0)
        indicator = (kinds == tokens).astype(jnp.float32).astype(jnp.bfloat16)
        embedded = local_ref[s].astype(jnp.float32) + dot(indicator, table_ref[...], TN)
        embedded_ref[s] = by_half(embedded)
        normed = normalize(embedded).astype(jnp.bfloat16)
        queries = dot(normed, row_wq[...]) * (HEAD_DIM ** -0.5 * LOG2E)
        query_ref[s] = by_half(queries).astype(jnp.bfloat16)
        key_ref[s] = dot(normed, row_wk[...]).astype(jnp.bfloat16)
        value_ref[s] = dot(normed, row_wv[...]).astype(jnp.bfloat16)
        gate_ref[s] = by_half(sigmoid(dot(normed, row_wg[...]))).astype(jnp.bfloat16)
        for which, k in RELAY_AFTER:
            pl.when(s == k)(functools.partial(run, relays[which]))

    real = residue_mask_ref[...] > 0
    pairs = sequences // 2
    pieces = pairs // PIECE

    def turn_copy(rows, target, slot, piece):
        span = pl.ds(piece * PIECE, PIECE)
        return pltpu.make_async_remote_copy(
            src_ref=updated_ref.at[rows, target, span], dst_ref=arrived_ref.at[rows, slot, span],
            send_sem=turn_send.at[rows, target, piece], recv_sem=turn_recv.at[rows, slot, piece],
            device_id={"dap": target}, device_id_type=MESH,
        )

    run(waits[0])

    @pl.loop(0, 2)
    def _(rows):
        pl.when(rows == 1)(functools.partial(run, waits[1]))

        for head in range(0, HEADS, 2):
            both = bias_ref[rows, :, ROWS * head:ROWS * (head + 2), :].astype(jnp.float32) * LOG2E
            for i in range(2):
                part = both[:, ROWS * i:ROWS * (i + 1), :].reshape(peers * ROWS, residues)
                wide_ref[head + i] = jnp.where(real, part, MASKED)

        @pl.loop(0, pieces)
        def _(piece):
            results = []
            for i in range(2 * PIECE):
                s = 2 * PIECE * piece + i
                attended = attend(
                    query_ref[s, rows],
                    lambda g: key_ref[s, :, 128 * g:128 * (g + 1)],
                    lambda g: value_ref[s, :, 128 * g:128 * (g + 1)],
                    lambda inner: jnp.broadcast_to(head_lanes(inner), (residues, 128)),
                    lambda head: wide_ref[head],
                )
                mixed = (attended * gate_ref[s, rows].astype(jnp.float32)).astype(jnp.bfloat16)
                updated = embedded_ref[s, rows] + dot(mixed, row_wo[...])
                results.append(updated.reshape(peers, ROWS, channels))
            for i in range(PIECE):
                p = piece * PIECE + i
                both = jnp.concatenate(results[2 * i:2 * i + 2], axis=1)
                updated_ref[rows, :, p] = both.astype(jnp.bfloat16)
                arrived_ref[rows, me, p] = updated_ref[rows, me, p]
            for step in range(1, peers):
                turn_copy(rows, (me + step) % peers, me, piece).start()

    tokens = 512
    lines = tokens // ROWS
    sources = lines // sequences
    everyone = peers * sequences
    real = jnp.broadcast_to(sequence_mask_ref[...].astype(jnp.float32), (128, everyone))
    real = jnp.transpose(real)
    for inner in range(GROUP):
        live_ref[inner] = real.astype(jnp.bfloat16) * head_lanes(inner)
    real = jnp.concatenate([real, real], axis=1)

    def span_of(i):
        return pl.ds(pl.multiple_of(i * tokens, tokens), tokens)

    for rows in range(2):
        @pl.loop(0, peers // sources)
        def _(i):
            for j in range(sources):
                source = i * sources + j

                @pl.when(source != me)
                def _():
                    for piece in range(pieces):
                        turn_copy(rows, source, source, piece).wait_recv()
            part = arrived_ref[rows, pl.ds(i * sources, sources)]
            part = part.astype(jnp.float32).reshape(tokens, channels)
            for half in range(2):
                column_ref[rows, half, span_of(i), :] = part[:, 128 * half:128 * (half + 1)]

        @pl.loop(0, ROWS // COLUMNS)
        def _(i):
            spans = [pl.ds(i * COLUMNS + j, everyone, stride=ROWS) for j in range(COLUMNS)]
            updated = jnp.concatenate([
                jnp.concatenate([column_ref[rows, half, span, :] for half in range(2)], axis=1)
                for span in spans
            ], axis=0)
            normed = normalize(updated).astype(jnp.bfloat16)
            queries = dot(normed, col_wq[...]) * (HEAD_DIM ** -0.5 * LOG2E)
            queries = queries.astype(jnp.bfloat16)
            all_keyed = dot(normed, col_wk[...])
            all_valued = dot(normed, col_wv[...])
            gate = sigmoid(dot(normed, col_wg[...]))
            results = []
            for j in range(COLUMNS):
                mine = slice(everyone * j, everyone * (j + 1))
                keyed = all_keyed[mine]
                keyed = jnp.where(real > 0.0, keyed, keyed[0:1, :]).astype(jnp.bfloat16)
                valued = (all_valued[mine] * real).astype(jnp.bfloat16)
                results.append(attend(
                    queries[mine],
                    lambda g: keyed[:, 128 * g:128 * (g + 1)],
                    lambda g: valued[:, 128 * g:128 * (g + 1)],
                    lambda inner: live_ref[inner],
                    None,
                ))
            mixed = (jnp.concatenate(results, axis=0) * gate).astype(jnp.bfloat16)
            result = updated + dot(mixed, col_wo[...])
            for j, span in enumerate(spans):
                mine = slice(everyone * j, everyone * (j + 1))
                for half in range(2):
                    column_ref[rows, half, span, :] = result[mine, 128 * half:128 * (half + 1)]

    @pl.loop(0, peers // sources)
    def _(i):
        both = []
        for rows in range(2):
            halves = [column_ref[rows, half, span_of(i), :] for half in range(2)]
            both.append(jnp.concatenate(halves, axis=1).reshape(lines, ROWS, channels))
        out_ref[pl.ds(pl.multiple_of(i * lines, lines), lines)] = (
            jnp.concatenate(both, axis=1).astype(jnp.bfloat16)
        )

    for send in sends:
        part, block, target = send
        gather_copy(part, at(block), at(target), number[send]).wait_send()

    @pl.loop(1, peers)
    def _(step):
        for rows in range(2):
            for piece in range(pieces):
                turn_copy(rows, (me + step) % peers, me, piece).wait_send()


def both_attentions(pair_state, pair_weight, state, tokens, residue_mask, sequence_mask, table, weights):
    sequences, residues, channels = state.shape
    rows_each = pair_state.shape[0]
    peers = residues // rows_each
    everyone = peers * sequences
    pairs = sequences // 2
    block = (2, peers, pairs, 2 * ROWS, channels)
    first, steps = gather_plan()
    count = len(first) + sum(len(step[2]) for step in steps)
    whole = pl.BlockSpec(memory_space=pltpu.VMEM)
    hbm = pl.BlockSpec(memory_space=pl.ANY)
    bf16, f32 = jnp.bfloat16, jnp.float32
    return pl.pallas_call(
        kernel,
        out_shape=jax.ShapeDtypeStruct((everyone, rows_each, channels), bf16),
        in_specs=[hbm, whole, hbm] + [whole] * 4 + [hbm] * WEIGHTS,
        out_specs=whole,
        scratch_shapes=[
            pltpu.VMEM(pair_state.shape, bf16),
            pltpu.VMEM((WEIGHTS, channels, channels), bf16),
            pltpu.VMEM((sequences, residues, channels), bf16),
            pltpu.VMEM((2, peers, HEADS * ROWS, residues), bf16),
            pltpu.VMEM((sequences, 2, peers * ROWS, channels), f32),
            pltpu.VMEM((sequences, 2, peers * ROWS, channels), bf16),
            pltpu.VMEM((sequences, residues, channels), bf16),
            pltpu.VMEM((sequences, residues, channels), bf16),
            pltpu.VMEM((sequences, 2, peers * ROWS, channels), bf16),
            pltpu.VMEM((HEADS, peers * ROWS, residues), f32),
            pltpu.VMEM(block, bf16),
            pltpu.VMEM(block, bf16),
            pltpu.VMEM((2, 2, everyone * ROWS, 128), f32),
            pltpu.VMEM((GROUP, everyone, 128), bf16),
            pltpu.SemaphoreType.DMA((3 + WEIGHTS,)),
            pltpu.SemaphoreType.DMA((count,)),
            pltpu.SemaphoreType.DMA((2, 2, peers)),
            pltpu.SemaphoreType.DMA((2, peers, pairs // PIECE)),
            pltpu.SemaphoreType.DMA((2, peers, pairs // PIECE)),
        ],
        compiler_params=pltpu.CompilerParams(
            vmem_limit_bytes=VMEM_LIMIT, collective_id=0, has_side_effects=True
        ),
        name="both_attentions",
    )(pair_state, pair_weight, state, tokens, residue_mask, sequence_mask, table, *weights)


def body(
    alignment_state,
    token_index_grid,
    sequence_mask,
    residue_mask,
    pair_state,
    token_embedding_table,
    pair_bias_weight,
    row_query_weight,
    row_key_weight,
    row_value_weight,
    row_gate_weight,
    row_output_weight,
    column_query_weight,
    column_key_weight,
    column_value_weight,
    column_gate_weight,
    column_output_weight,
):
    return both_attentions(
        pair_state, pair_bias_weight.T, alignment_state, token_index_grid, residue_mask[None, :],
        sequence_mask[None, :], token_embedding_table,
        (row_query_weight, row_key_weight, row_value_weight, row_gate_weight, row_output_weight,
         column_query_weight, column_key_weight, column_value_weight, column_gate_weight,
         column_output_weight),
    )


def solution(mesh):
    split = P(("dp", "dap"), None, None)
    in_specs = (
        split, P(("dp", "dap"), None), P("dp"), P("dp"), split,
    ) + (P(),) * 12
    return jax.shard_map(
        body, mesh=mesh, in_specs=in_specs, out_specs=P("dp", "dap", None), check_vma=False
    )
```

```python
import functools

import jax
import jax.numpy as jnp
from jax import lax
from jax.experimental import pallas as pl
from jax.experimental.pallas import tpu as pltpu
from jax.sharding import PartitionSpec as P

HEADS = 8
HEAD_DIM = 32
GROUP = 4
TOKEN_KINDS = 23
EPSILON = 1e-05
LOG2E = 1.4426950408889634
MASKED = -1e9
ROWS = 8
PIECE = 2
WEIGHTS = 10
COLUMNS = 8
RELAY_AFTER = (((0, 1), 0), ((1, 0), 1), ((1, 1), 2))
XS, ZS, YS = 4, 2, 4
MESH = pl.DeviceIdType.MESH
VMEM_LIMIT = 60 * 1024 * 1024

NT = (((1,), (1,)), ((), ()))
TN = (((0,), (0,)), ((), ()))


def dot(a, b, dims=(((1,), (0,)), ((), ()))):
    return lax.dot_general(a, b, dims, preferred_element_type=jnp.float32)


def normalize(values):
    centered = values - jnp.mean(values, axis=-1, keepdims=True)
    variance = jnp.mean(centered * centered, axis=-1, keepdims=True)
    return centered * lax.rsqrt(variance + EPSILON)


def sigmoid(x):
    return 0.5 * jnp.tanh(0.5 * x) + 0.5


def lane_head(shape):
    return lax.broadcasted_iota(jnp.int32, shape, len(shape) - 1) // HEAD_DIM


def head_lanes(inner):
    return (lane_head((1, 128)) == inner).astype(jnp.float32).astype(jnp.bfloat16)


def attend(queries, key_at, value_at, ones_at, bias_at):
    halves = []
    for group in range(HEADS // GROUP):
        q = queries[:, 128 * group:128 * (group + 1)]
        keyed, valued = key_at(group), value_at(group)
        all_probs, all_values = [], []
        for inner in range(GROUP):
            mine = head_lanes(inner)
            scores = dot(q, keyed * mine, NT)
            if bias_at is not None:
                scores = scores + bias_at(group * GROUP + inner)
            top = jnp.max(scores, axis=-1, keepdims=True)
            all_probs.append(jnp.exp2(scores - top).astype(jnp.bfloat16))
            all_values.append(jnp.concatenate([valued * mine, ones_at(inner)], axis=1))
        total = dot(jnp.concatenate(all_probs, axis=1), jnp.concatenate(all_values, axis=0))
        halves.append(total[:, 0:128] / total[:, 128:256])
    return jnp.concatenate(halves, axis=1)


def gather_plan():
    def place(half, u, z, v):
        return (v % XS, z % ZS, u % YS) if half == 0 else (u % XS, z % ZS, v % YS)

    first, steps = [], []
    for rows in range(2):
        for half in range(2):
            part = (rows, half)
            for target in ((1, 0, 0), (-1, 0, 0), (2, 0, 0), (0, 1, 0), (0, 0, 1), (0, 0, -1), (0, 0, 2)):
                first.append((part, (0, 0, 0), place(half, *target)))
            for u in (0, 1, -1, 2):
                for z in range(2):
                    for v in (0, 1, -1, 2):
                        if (u, z, v) == (0, 0, 0):
                            continue
                        to = []
                        if v == 0 and z == 0:
                            to.append((0, 1, 0))
                        if v == 0:
                            to += [(0, 0, 1), (0, 0, -1), (0, 0, 2)]
                        hops = abs(u) + abs(v) + 1.5 * z
                        order = hops
                        steps.append((order, part, place(half, u, z, v), [place(half, *t) for t in to]))
    steps.sort(key=lambda step: step[:3])
    return first, [step[1:] for step in steps]


def split_steps(steps):
    relays = {(rows, level): [] for rows in range(2) for level in range(2)}
    waits = ([], [])
    for step in steps:
        (rows, _), block, to = step
        if to:
            relays[rows, block[1]].append(step)
        else:
            waits[rows].append(step)
    return relays, waits


def kernel(
    pair_hbm, pair_weight_ref, state_ref, token_ref, residue_mask_ref, sequence_mask_ref, table_ref,
    *refs,
):
    weights_hbm, refs = refs[:WEIGHTS], refs[WEIGHTS:]
    (
        out_ref,
        pair_ref, weights_ref, local_ref, bias_ref, embedded_ref, query_ref, key_ref, value_ref, gate_ref, wide_ref,
        updated_ref, arrived_ref, column_ref, live_ref,
        local_sem, gather_send, gather_recv, turn_send, turn_recv,
    ) = refs
    sequences, residues, channels = local_ref.shape
    rows_each, _, pair_channels = pair_ref.shape
    peers = residues // rows_each
    me = lax.axis_index("dap")
    x, z, y = me // (ZS * YS), (me // YS) % ZS, me % YS

    def at(offset):
        dx, dz, dy = offset
        return (((x + dx) % XS) * ZS + (z + dz) % ZS) * YS + (y + dy) % YS

    half_rows = [pl.ds(ROWS * rows, ROWS) for rows in range(2)]
    load_pair = [
        pltpu.make_async_copy(pair_hbm.at[half_rows[i]], pair_ref.at[half_rows[i]], local_sem.at[i])
        for i in range(2)
    ]
    load = pltpu.make_async_copy(state_ref, local_ref, local_sem.at[2])
    load_weights = [
        pltpu.make_async_copy(weights_hbm[i], weights_ref.at[i], local_sem.at[3 + i])
        for i in range(WEIGHTS)
    ]
    for copy in load_pair + [load] + load_weights:
        copy.start()
    row_wq, row_wk, row_wv, row_wg, row_wo = [weights_ref.at[i] for i in range(5)]
    col_wq, col_wk, col_wv, col_wg, col_wo = [weights_ref.at[i] for i in range(5, WEIGHTS)]
    barrier = pltpu.get_barrier_semaphore()
    for step in range(1, peers):
        pl.semaphore_signal(
            barrier, inc=1, device_id={"dap": (me + step) % peers}, device_id_type=MESH
        )

    first, steps = gather_plan()
    sends = first + [(part, block, target) for part, block, to in steps for target in to]
    number = {send: i for i, send in enumerate(sends)}

    def gather_copy(part, block, target, index):
        rows, half = part
        piece = bias_ref.at[rows, block, pl.ds(half * (HEADS // 2) * ROWS, HEADS // 2 * ROWS)]
        return pltpu.make_async_remote_copy(
            src_ref=piece, dst_ref=piece,
            send_sem=gather_send.at[index], recv_sem=gather_recv.at[rows, half, block],
            device_id={"dap": target}, device_id_type=MESH,
        )

    def start(send):
        part, block, target = send
        gather_copy(part, at(block), at(target), number[send]).start()

    def run(steps):
        for part, block, to in steps:
            gather_copy(part, at(block), at((0, 1, 0)), 0).wait_recv()
            for target in to:
                start((part, block, target))

    averaging = jnp.full((pair_channels, pair_channels), 1.0 / pair_channels, jnp.bfloat16)
    spread = pair_weight_ref[...].astype(jnp.float32)
    spread = jnp.broadcast_to(spread[:, None, :], (HEADS, ROWS, pair_channels))
    spread = spread.reshape(HEADS * ROWS, pair_channels)
    row_of = lax.broadcasted_iota(jnp.int32, spread.shape, 0) % ROWS
    for rows in range(2):
        load_pair[rows].wait()
        total = None
        for row in range(ROWS):
            block = pair_ref[rows * ROWS + row]
            centered = block.astype(jnp.float32) - dot(block, averaging)
            variance = dot((centered * centered).astype(jnp.bfloat16), averaging)
            normed = (centered * lax.rsqrt(variance + EPSILON)).astype(jnp.bfloat16)
            weight = jnp.where(row_of == row, spread, 0.0).astype(jnp.bfloat16)
            product = dot(weight, normed, NT)
            total = product if total is None else total + product
        bias_ref[rows, me] = total.astype(jnp.bfloat16)
        if rows == 0:
            pl.semaphore_wait(barrier, peers - 1)
        for send in first:
            if send[0][0] == rows:
                start(send)

    relays, waits = split_steps(steps)
    run(relays[0, 0])
    load.wait()
    for copy in load_weights:
        copy.wait()

    def by_half(values):
        return jnp.swapaxes(values.reshape(peers, 2, ROWS, channels), 0, 1).reshape(
            2, peers * ROWS, channels
        )

    @pl.loop(0, sequences // 2)
    def _(pair):
        for s in (2 * pair, 2 * pair + 1):
            tokens = token_ref[pl.ds(s, 1), :]
            kinds = lax.broadcasted_iota(jnp.int32, (TOKEN_KINDS, residues), 0)
            indicator = (kinds == tokens).astype(jnp.float32).astype(jnp.bfloat16)
            embedded = local_ref[s].astype(jnp.float32) + dot(indicator, table_ref[...], TN)
            embedded_ref[s] = by_half(embedded)
            normed = normalize(embedded).astype(jnp.bfloat16)
            queries = dot(normed, row_wq[...]) * (HEAD_DIM ** -0.5 * LOG2E)
            query_ref[s] = by_half(queries).astype(jnp.bfloat16)
            key_ref[s] = dot(normed, row_wk[...]).astype(jnp.bfloat16)
            value_ref[s] = dot(normed, row_wv[...]).astype(jnp.bfloat16)
            gate_ref[s] = by_half(sigmoid(dot(normed, row_wg[...]))).astype(jnp.bfloat16)
        for which, k in RELAY_AFTER:
            pl.when(pair == k)(functools.partial(run, relays[which]))

    real = residue_mask_ref[...] > 0
    pairs = sequences // 2
    pieces = pairs // PIECE

    def turn_copy(rows, target, slot, piece):
        span = pl.ds(piece * PIECE, PIECE)
        return pltpu.make_async_remote_copy(
            src_ref=updated_ref.at[rows, target, span], dst_ref=arrived_ref.at[rows, slot, span],
            send_sem=turn_send.at[rows, target, piece], recv_sem=turn_recv.at[rows, slot, piece],
            device_id={"dap": target}, device_id_type=MESH,
        )

    run(waits[0])

    @pl.loop(0, 2)
    def _(rows):
        pl.when(rows == 1)(functools.partial(run, waits[1]))

        for head in range(0, HEADS, 2):
            both = bias_ref[rows, :, ROWS * head:ROWS * (head + 2), :].astype(jnp.float32) * LOG2E
            for i in range(2):
                part = both[:, ROWS * i:ROWS * (i + 1), :].reshape(peers * ROWS, residues)
                wide_ref[head + i] = jnp.where(real, part, MASKED)

        @pl.loop(0, pieces)
        def _(piece):
            results = []
            for i in range(2 * PIECE):
                s = 2 * PIECE * piece + i
                attended = attend(
                    query_ref[s, rows],
                    lambda g: key_ref[s, :, 128 * g:128 * (g + 1)],
                    lambda g: value_ref[s, :, 128 * g:128 * (g + 1)],
                    lambda inner: jnp.broadcast_to(head_lanes(inner), (residues, 128)),
                    lambda head: wide_ref[head],
                )
                mixed = (attended * gate_ref[s, rows].astype(jnp.float32)).astype(jnp.bfloat16)
                updated = embedded_ref[s, rows] + dot(mixed, row_wo[...])
                results.append(updated.reshape(peers, ROWS, channels))
            for i in range(PIECE):
                p = piece * PIECE + i
                both = jnp.concatenate(results[2 * i:2 * i + 2], axis=1)
                updated_ref[rows, :, p] = both.astype(jnp.bfloat16)
                arrived_ref[rows, me, p] = updated_ref[rows, me, p]
            for step in range(1, peers):
                turn_copy(rows, (me + step) % peers, me, piece).start()

    tokens = 512
    lines = tokens // ROWS
    sources = lines // sequences
    everyone = peers * sequences
    real = jnp.broadcast_to(sequence_mask_ref[...].astype(jnp.float32), (128, everyone))
    real = jnp.transpose(real)
    for inner in range(GROUP):
        live_ref[inner] = real.astype(jnp.bfloat16) * head_lanes(inner)
    real = jnp.concatenate([real, real], axis=1)

    def span_of(i):
        return pl.ds(pl.multiple_of(i * tokens, tokens), tokens)

    for rows in range(2):
        @pl.loop(0, peers // sources)
        def _(i):
            for j in range(sources):
                source = i * sources + j

                @pl.when(source != me)
                def _():
                    for piece in range(pieces):
                        turn_copy(rows, source, source, piece).wait_recv()
            part = arrived_ref[rows, pl.ds(i * sources, sources)]
            part = part.astype(jnp.float32).reshape(tokens, channels)
            for half in range(2):
                column_ref[rows, half, span_of(i), :] = part[:, 128 * half:128 * (half + 1)]

        @pl.loop(0, ROWS // COLUMNS)
        def _(i):
            spans = [pl.ds(i * COLUMNS + j, everyone, stride=ROWS) for j in range(COLUMNS)]
            updated = jnp.concatenate([
                jnp.concatenate([column_ref[rows, half, span, :] for half in range(2)], axis=1)
                for span in spans
            ], axis=0)
            normed = normalize(updated).astype(jnp.bfloat16)
            queries = dot(normed, col_wq[...]) * (HEAD_DIM ** -0.5 * LOG2E)
            queries = queries.astype(jnp.bfloat16)
            all_keyed = dot(normed, col_wk[...])
            all_valued = dot(normed, col_wv[...])
            gate = sigmoid(dot(normed, col_wg[...]))
            results = []
            for j in range(COLUMNS):
                mine = slice(everyone * j, everyone * (j + 1))
                keyed = all_keyed[mine]
                keyed = jnp.where(real > 0.0, keyed, keyed[0:1, :]).astype(jnp.bfloat16)
                valued = (all_valued[mine] * real).astype(jnp.bfloat16)
                results.append(attend(
                    queries[mine],
                    lambda g: keyed[:, 128 * g:128 * (g + 1)],
                    lambda g: valued[:, 128 * g:128 * (g + 1)],
                    lambda inner: live_ref[inner],
                    None,
                ))
            mixed = (jnp.concatenate(results, axis=0) * gate).astype(jnp.bfloat16)
            result = updated + dot(mixed, col_wo[...])
            for j, span in enumerate(spans):
                mine = slice(everyone * j, everyone * (j + 1))
                for half in range(2):
                    column_ref[rows, half, span, :] = result[mine, 128 * half:128 * (half + 1)]

    @pl.loop(0, peers // sources)
    def _(i):
        both = []
        for rows in range(2):
            halves = [column_ref[rows, half, span_of(i), :] for half in range(2)]
            both.append(jnp.concatenate(halves, axis=1).reshape(lines, ROWS, channels))
        out_ref[pl.ds(pl.multiple_of(i * lines, lines), lines)] = (
            jnp.concatenate(both, axis=1).astype(jnp.bfloat16)
        )

    for send in sends:
        part, block, target = send
        gather_copy(part, at(block), at(target), number[send]).wait_send()

    @pl.loop(1, peers)
    def _(step):
        for rows in range(2):
            for piece in range(pieces):
                turn_copy(rows, (me + step) % peers, me, piece).wait_send()


def both_attentions(pair_state, pair_weight, state, tokens, residue_mask, sequence_mask, table, weights):
    sequences, residues, channels = state.shape
    rows_each = pair_state.shape[0]
    peers = residues // rows_each
    everyone = peers * sequences
    pairs = sequences // 2
    block = (2, peers, pairs, 2 * ROWS, channels)
    first, steps = gather_plan()
    count = len(first) + sum(len(step[2]) for step in steps)
    whole = pl.BlockSpec(memory_space=pltpu.VMEM)
    hbm = pl.BlockSpec(memory_space=pl.ANY)
    bf16, f32 = jnp.bfloat16, jnp.float32
    return pl.pallas_call(
        kernel,
        out_shape=jax.ShapeDtypeStruct((everyone, rows_each, channels), bf16),
        in_specs=[hbm, whole, hbm] + [whole] * 4 + [hbm] * WEIGHTS,
        out_specs=whole,
        scratch_shapes=[
            pltpu.VMEM(pair_state.shape, bf16),
            pltpu.VMEM((WEIGHTS, channels, channels), bf16),
            pltpu.VMEM((sequences, residues, channels), bf16),
            pltpu.VMEM((2, peers, HEADS * ROWS, residues), bf16),
            pltpu.VMEM((sequences, 2, peers * ROWS, channels), f32),
            pltpu.VMEM((sequences, 2, peers * ROWS, channels), bf16),
            pltpu.VMEM((sequences, residues, channels), bf16),
            pltpu.VMEM((sequences, residues, channels), bf16),
            pltpu.VMEM((sequences, 2, peers * ROWS, channels), bf16),
            pltpu.VMEM((HEADS, peers * ROWS, residues), f32),
            pltpu.VMEM(block, bf16),
            pltpu.VMEM(block, bf16),
            pltpu.VMEM((2, 2, everyone * ROWS, 128), f32),
            pltpu.VMEM((GROUP, everyone, 128), bf16),
            pltpu.SemaphoreType.DMA((3 + WEIGHTS,)),
            pltpu.SemaphoreType.DMA((count,)),
            pltpu.SemaphoreType.DMA((2, 2, peers)),
            pltpu.SemaphoreType.DMA((2, peers, pairs // PIECE)),
            pltpu.SemaphoreType.DMA((2, peers, pairs // PIECE)),
        ],
        compiler_params=pltpu.CompilerParams(
            vmem_limit_bytes=VMEM_LIMIT, collective_id=0, has_side_effects=True
        ),
        name="both_attentions",
    )(pair_state, pair_weight, state, tokens, residue_mask, sequence_mask, table, *weights)


def body(
    alignment_state,
    token_index_grid,
    sequence_mask,
    residue_mask,
    pair_state,
    token_embedding_table,
    pair_bias_weight,
    row_query_weight,
    row_key_weight,
    row_value_weight,
    row_gate_weight,
    row_output_weight,
    column_query_weight,
    column_key_weight,
    column_value_weight,
    column_gate_weight,
    column_output_weight,
):
    return both_attentions(
        pair_state, pair_bias_weight.T, alignment_state, token_index_grid, residue_mask[None, :],
        sequence_mask[None, :], token_embedding_table,
        (row_query_weight, row_key_weight, row_value_weight, row_gate_weight, row_output_weight,
         column_query_weight, column_key_weight, column_value_weight, column_gate_weight,
         column_output_weight),
    )


def solution(mesh):
    split = P(("dp", "dap"), None, None)
    in_specs = (
        split, P(("dp", "dap"), None), P("dp"), P("dp"), split,
    ) + (P(),) * 12
    return jax.shard_map(
        body, mesh=mesh, in_specs=in_specs, out_specs=P("dp", "dap", None), check_vma=False
    )
```
